128 devices in a mesh: span: 32 (over z, x, core), real: 4 (over y).
Axes of the slice: x: 4, y: 4, z: 4, core: 2. Of those that a mesh axis runs over, the one named last changes fastest.
Arguments:
- snapshots: float32 [8, 64, 512, 256], P('real', 'span'), may hold values from -10 to 10
- load: float32 [64, 512, 256], P('span'), may hold values from -6 to 6
- base_modulus: float32 [64, 512, 256], P('span'), may hold values from 0.5 to 2
- mistune: float32 [8], replicated, may hold values from 0.5 to 2
- material_ids: int32 [8, 32], replicated, may hold values from 0 to 7
- realization_map: int32 [8], P('real'), may hold values from 0 to 7, each once
- picks: int32 [2], replicated, may hold values from 0 to 7, as said below
Outputs:
- reduced_matrices: float32 [8, 2, 2], P('real')
- residual_fields: float32 [8, 64, 512, 256], P('real', 'span')
- residual_norms: float32 [8], P('real')
The draws below stay inside these ranges and needn't reach their ends.
Inputs may be any that keep to these rules, and one draw needn't show every extreme that they name: `picks`: the two chosen snapshot indices differ, and one of them is the last snapshot, 7.
All inputs are finite; a program needn't handle non-finite values.
Results may differ from the reference program's by a relative error of at most 0.000075.
Values sent between devices are 32-bit elements; how exact they have to be, the bound alone decides.
A program may use at most 256 MiB of HBM per device.

```python
import math
import jax
import jax.numpy as jnp
from jax import lax

NC = 512
NA = 256
SECTORS = 32
NMAT = 8
NS = 64
R = 8
S = 8


def load_field(key):
    inner_key = jax.random.fold_in(key, 11)
    raw_field = jax.random.truncated_normal(inner_key, -4.0, 4.0, (NS, NC, NA), jnp.float32)
    ramp_scale = 0.5 + jnp.arange(NS, dtype=jnp.float32) / NS
    return raw_field * ramp_scale[:, None, None]


def draw_load(key, part):
    return load_field(key)


def draw_snapshots(key, part):
    base_load = load_field(key)
    gains = jax.random.uniform(jax.random.fold_in(key, 12), (S,), jnp.float32, 0.3, 1.0)
    noise_field = jax.random.truncated_normal(jax.random.fold_in(key, 13), -4.0, 4.0, (S, NS, NC, NA), jnp.float32)
    return gains[:, None, None, None] * base_load[None] + noise_field


def draw_picks(key, part):
    key = jax.random.fold_in(key, 21)
    other_pick = jax.random.randint(jax.random.fold_in(key, 1), (), 0, S - 1).astype(jnp.int32)
    last_pick = jnp.array(S - 1, jnp.int32)
    order_bit = jax.random.randint(jax.random.fold_in(key, 2), (), 0, 2).astype(jnp.int32)
    first = jnp.where(order_bit == 0, other_pick, last_pick)
    second = jnp.where(order_bit == 0, last_pick, other_pick)
    return jnp.stack([first, second]).astype(jnp.int32)


def plant(drawn, key, smallest, high):
    longest = drawn.shape.index(max(drawn.shape))
    spots = []
    for shift in (0, 1):
        where = [jax.random.randint(jax.random.fold_in(key, axis), (), 0, length) for axis, length in enumerate(drawn.shape)]
        where[longest] = (where[longest] + shift) % drawn.shape[longest]
        spots.append(tuple(where))
    return drawn.at[spots[0]].set(smallest).at[spots[1]].set(high)


def block_scale(rng, extent, cuts, low, top_value):
    def one(axis_at, shards_of):
        draws = jax.random.uniform(jax.random.fold_in(jax.random.fold_in(rng, 6), axis_at), (shards_of,), jnp.float32, low / len(cuts), top_value / len(cuts))
        return jnp.repeat(jnp.exp(draws), extent[axis_at] // shards_of).reshape((-1,) + (1,) * (len(extent) - axis_at - 1))

    factor_of = one(*cuts[0])
    for cut in cuts[1:]:
        factor_of = factor_of * one(*cut)
    return factor_of


def setup_inputs(seed: int = 0) -> dict:
    splits = jax.random.split(jax.random.key(seed), 8)
    return {
        "snapshots": draw_snapshots(jax.random.fold_in(splits[7], 71), 0),
        "load": draw_load(jax.random.fold_in(splits[7], 71), 0),
        "base_modulus": jnp.clip(jnp.exp(math.log(2.0) - 1.3862944 * jax.random.uniform(splits[2], (NS, NC, NA), jnp.float32) ** block_scale(splits[2], (NS, NC, NA), ((0, 32),), -0.2, 0.2)), 0.5, 2.0),
        "mistune": jnp.clip(jnp.exp(jax.random.uniform(splits[3], (NMAT,), jnp.float32, math.log(0.5), math.log(2.0))), 0.5, 2.0),
        "material_ids": plant(jax.random.randint(splits[4], (R, SECTORS), 0, NMAT), jax.random.fold_in(splits[4], 1), 0, NMAT - 1).astype(jnp.int32),
        "realization_map": jax.random.permutation(splits[5], R).astype(jnp.int32),
        "picks": draw_picks(jax.random.fold_in(splits[7], 71), 0),
    }


mass_shift = 0.5
self_weight = 14.0

def stencil_offsets():
    offsets = []
    for span_off in (-1, 0, 1):
        for circ_off in (-1, 0, 1):
            for axial_off in (-1, 0, 1):
                moved = abs(span_off) + abs(circ_off) + abs(axial_off)
                if moved > 0:
                    offsets.append((span_off, circ_off, axial_off, 1.0 / 2 ** (moved - 1)))
    return offsets

def neighbour_sum(padded):
    length = padded.shape[-3] - 2
    width = padded.shape[-1]
    widened = jnp.pad(padded, [(0, 0)] * (padded.ndim - 1) + [(1, 1)])
    weighted = jnp.zeros(padded.shape[:-3] + (length, padded.shape[-2], width), padded.dtype)
    for span_off, circ_off, axial_off, weight in stencil_offsets():
        shifted = widened[..., 1 + span_off:1 + span_off + length, :, 1 + axial_off:1 + axial_off + width]
        if circ_off != 0:
            shifted = jnp.roll(shifted, -circ_off, axis=-2)
        weighted = weighted + weight * shifted
    return weighted

def apply_stiffness(modulus, root_field, padded, basis):
    center = padded[..., 1:-1, :, :]
    return mass_shift * modulus * basis + root_field * (self_weight * center - neighbour_sum(padded))

def circ_factors(material_ids, mistune, rows):
    chosen = jnp.take(material_ids, rows, axis=0)
    onehot = (chosen[:, :, None] == jnp.arange(mistune.shape[0], dtype=jnp.int32)[None, None, :]).astype(jnp.float32)
    sector_factor = lax.optimization_barrier(jnp.sum(onehot * mistune.astype(jnp.float32)[None, None, :], axis=-1))
    return jnp.repeat(sector_factor, NC // SECTORS, axis=1)

def reference(snapshots, load, base_modulus, mistune, material_ids, realization_map, picks):
    cell_count = float(NS * NC * NA)
    first_slab = lax.dynamic_index_in_dim(snapshots, picks[0], 0, keepdims=False)
    norm_first = jnp.sum(first_slab * first_slab) / cell_count
    basis_zero = first_slab / jnp.sqrt(norm_first)
    second_slab = lax.dynamic_index_in_dim(snapshots, picks[1], 0, keepdims=False)
    projected = jnp.sum(basis_zero * second_slab) / cell_count
    remainder = second_slab - projected * basis_zero
    norm_second = jnp.sum(remainder * remainder) / cell_count
    basis_one = remainder / jnp.sqrt(norm_second)
    load_zero = jnp.sum(basis_zero * load) / cell_count
    load_one = jnp.sum(basis_one * load) / cell_count
    factors = circ_factors(material_ids, mistune, realization_map)

    def one_realization(circ_factor):
        modulus = base_modulus * circ_factor[None, :, None]
        root_field = jnp.sqrt(modulus)

        def stiffen(basis):
            padded = jnp.pad(root_field * basis, ((1, 1), (0, 0), (0, 0)))
            return apply_stiffness(modulus, root_field, padded, basis)
        image_zero = stiffen(basis_zero)
        image_one = stiffen(basis_one)
        entry_aa = jnp.sum(basis_zero * image_zero) / cell_count
        entry_ab = jnp.sum(basis_zero * image_one) / cell_count
        entry_bb = jnp.sum(basis_one * image_one) / cell_count
        determinant = entry_aa * entry_bb - entry_ab * entry_ab
        coeff_zero = (entry_bb * load_zero - entry_ab * load_one) / determinant
        coeff_one = (entry_aa * load_one - entry_ab * load_zero) / determinant
        residual_field = load - coeff_zero * image_zero - coeff_one * image_one
        reduced = jnp.stack([jnp.stack([entry_aa, entry_ab]), jnp.stack([entry_ab, entry_bb])])
        return (reduced, residual_field, jnp.sum(residual_field * residual_field) / cell_count)
    reduced_matrices, residual_fields, residual_norms = lax.map(one_realization, factors)
    return (reduced_matrices, residual_fields, residual_norms)
```

```python
import functools

import jax
import jax.numpy as jnp
from jax import lax
from jax.experimental import pallas as pl
from jax.experimental.pallas import tpu as pltpu
from jax.sharding import PartitionSpec as P

MESH = pl.DeviceIdType.MESH
SHIFT = 0.5
ROWS = 32
LAG = 1
PAD = 8
LANES = 128
F32 = jnp.float32


def kernel(
    owner, picks, mistune, ids, slots, snaps, load_in, base_in,
    red, res, nrm,
    field, edge, both, load, root, root_edge, mixed, image, factor, pair, totals, near, far,
    local_sem, send_sem, recv_sem, edge_send, edge_recv, root_send, root_recv,
    near_send, near_recv, far_send, far_recv,
):
    n_span, n_real = lax.axis_size("span"), lax.axis_size("real")
    span, real = lax.axis_index("span"), lax.axis_index("real")
    held, planes, circ, axial = snaps.shape
    sectors = ids.shape[1]
    width = circ // sectors
    pieces = circ // ROWS
    last = held * n_real - 1
    owners = (owner, n_real - 1)
    cells = float(planes * n_span * circ * axial)
    n_near, n_far = near.shape[0], far.shape[0]

    before, after = lax.rem(span + n_span - 1, n_span), lax.rem(span + 1, n_span)
    below, above = lax.rem(real + n_real - 1, n_real), lax.rem(real + 1, n_real)
    my_far, my_near = lax.div(span, n_near), lax.rem(span, n_near)

    def near_peer(i):
        return my_far * n_near + lax.rem(my_near + i, n_near)

    def far_peer(i):
        return lax.rem(my_far + i, n_far) * n_near + my_near

    barrier = pltpu.get_barrier_semaphore()
    greeted = 0
    for where in [{"real": below}, {"real": above}, {"span": before}, {"span": after}]:
        pl.semaphore_signal(barrier, inc=1, device_id=where, device_id_type=MESH)
        greeted += 1
    for i in range(1, n_near):
        pl.semaphore_signal(barrier, inc=1, device_id={"span": near_peer(i)}, device_id_type=MESH)
        greeted += 1
    for i in range(1, n_far):
        pl.semaphore_signal(barrier, inc=1, device_id={"span": far_peer(i)}, device_id_type=MESH)
        greeted += 1

    base_copy = pltpu.make_async_copy(base_in, root, local_sem.at[0])
    load_copy = pltpu.make_async_copy(load_in, load, local_sem.at[1])
    last_copy = pltpu.make_async_copy(snaps.at[held - 1], field.at[1], local_sem.at[2])
    if owner == n_real - 1:
        other_copy = pltpu.make_async_copy(snaps.at[0], field.at[0], local_sem.at[3])
    else:
        other_copy = pltpu.make_async_copy(snaps, both, local_sem.at[3])

    @pl.when(real == owner)
    def _():
        other_copy.start()

    @pl.when(real == n_real - 1)
    def _():
        last_copy.start()

    base_copy.start()
    load_copy.start()

    def fill(j, carry):
        for t in range(2):
            value = mistune[ids[slots[t], j]]
            factor[t, pl.ds(PAD + j * width, width), :] = jnp.full((width, LANES), value, F32)
        return carry

    lax.fori_loop(0, sectors, fill, 0)
    for t in range(2):
        factor[t, 0:PAD, :] = factor[t, circ : circ + PAD, :]
        factor[t, circ + PAD : circ + 2 * PAD, :] = factor[t, PAD : 2 * PAD, :]
        here = factor[t, PAD : circ + PAD, :]
        for side, shift in ((0, -1), (1, 1)):
            pair[t, side] = jnp.sqrt(here * factor[t, PAD + shift : circ + PAD + shift, :])
    totals[...] = jnp.zeros_like(totals)

    @pl.when(real == owner)
    def _():
        other_copy.wait()
        if owner != n_real - 1:
            chosen = lax.rem(jnp.minimum(picks[0], picks[1]), held)

            def choose(i, carry):
                rows = pl.ds(pl.multiple_of(i * 16, 16), 16)
                for p in range(planes):
                    field[0, p, rows, :] = jnp.where(chosen == 0, both[0, p, rows, :], both[1, p, rows, :])
                return carry

            lax.fori_loop(0, circ // 16, choose, 0)

    @pl.when(real == n_real - 1)
    def _():
        last_copy.wait()

    base_copy.wait()

    def take_root(i, carry):
        rows = pl.ds(pl.multiple_of(i * 16, 16), 16)
        for p in range(planes):
            root[p, rows, :] = jnp.sqrt(root[p, rows, :])
        return carry

    lax.fori_loop(0, circ // 16, take_root, 0)
    pl.semaphore_wait(barrier, greeted)

    def root_hop(p):
        return pltpu.make_async_remote_copy(
            src_ref=root.at[p],
            dst_ref=root_edge.at[1 - p],
            send_sem=root_send.at[p],
            recv_sem=root_recv.at[1 - p],
            device_id={"span": before if p == 0 else after},
            device_id_type=MESH,
        )

    for p in range(2):
        root_hop(p).start()

    def rows_of(k):
        return pl.ds(pl.multiple_of(k * ROWS, ROWS), ROWS)

    def hop(s, p, k):
        return pltpu.make_async_remote_copy(
            src_ref=field.at[s, p, rows_of(k)],
            dst_ref=field.at[s, p, rows_of(k)],
            send_sem=send_sem.at[s, p],
            recv_sem=recv_sem.at[s, p, k],
            device_id={"real": above if p == 0 else below},
            device_id_type=MESH,
        )

    def edge_hop(s, p, k):
        return pltpu.make_async_remote_copy(
            src_ref=field.at[s, p, rows_of(k)],
            dst_ref=edge.at[s, 1 - p, rows_of(k)],
            send_sem=edge_send.at[s, p],
            recv_sem=edge_recv.at[s, 1 - p, k],
            device_id={"span": before if p == 0 else after},
            device_id_type=MESH,
        )

    distance = [
        (lax.rem(real + n_real - owners[s], n_real), lax.rem(owners[s] + n_real - real, n_real)) for s in range(2)
    ]

    low = jnp.where(span > 0, 0.5, 0.0).astype(F32)
    high = jnp.where(span < n_span - 1, 0.5, 0.0).astype(F32)
    column = lax.broadcasted_iota(jnp.int32, (8, axial), 1)
    not_first, not_last = column > 0, column < axial - 1

    def mix(k, carry):
        start = pl.multiple_of(k * 8, 8)
        rows = pl.ds(start, 8)
        q0, q1, ql, qh = root[0, rows, :], root[1, rows, :], root_edge[0, rows, :], root_edge[1, rows, :]
        for s in range(2):
            w0, w1 = q0 * field[s, 0, rows, :], q1 * field[s, 1, rows, :]
            wl, wh = ql * edge[s, 0, rows, :], qh * edge[s, 1, rows, :]
            for p, across in ((0, w0 + (low * wl + 0.5 * w1)), (1, w1 + (high * wh + 0.5 * w0))):
                left = jnp.where(not_first, pltpu.roll(across, 1, 1), 0.0)
                right = jnp.where(not_last, pltpu.roll(across, axial - 1, 1), 0.0)
                mixed[s, p, pl.ds(start + PAD, 8), :] = across + 0.5 * (left + right)
        return carry

    def fold(x):
        return x[:, :LANES] + x[:, LANES:]

    def work(j, carry):
        parts = [None] * 22

        def add(i, x):
            x = fold(x)
            parts[i] = x if parts[i] is None else parts[i] + x

        for h in range(width // 8):
            start = pl.multiple_of(j * width + h * 8, 8)
            rows = pl.ds(start, 8)
            wide = lambda x: jnp.concatenate([x] * (axial // LANES), axis=1)
            fac = [wide(factor[t, pl.ds(start + PAD, 8), :]) for t in range(2)]
            prev = [wide(pair[t, 0, rows, :]) for t in range(2)]
            succ = [wide(pair[t, 1, rows, :]) for t in range(2)]
            for p in range(planes):
                q, force = root[p, rows, :], load[p, rows, :]
                x0, x1 = field[0, p, rows, :], field[1, p, rows, :]
                images = [[None, None], [None, None]]
                for s, x in ((0, x0), (1, x1)):
                    tall = mixed[s, p, pl.ds(start + PAD - 8, 24), :]
                    up, centre, down = tall[7:15], tall[8:16], tall[9:17]
                    inner = (16.0 + SHIFT) * (q * x) - 2.0 * centre
                    for t in range(2):
                        im = q * (fac[t] * inner - (prev[t] * up + succ[t] * down))
                        image[t, s, p, rows, :] = im
                        images[t][s] = im
                for t in range(2):
                    i0, i1 = images[t]
                    add(8 * t + 0, x0 * i0)
                    add(8 * t + 1, x0 * i1)
                    add(8 * t + 2, x1 * i1)
                    add(8 * t + 3, force * i0)
                    add(8 * t + 4, force * i1)
                    add(8 * t + 5, i0 * i0)
                    add(8 * t + 6, i0 * i1)
                    add(8 * t + 7, i1 * i1)
                add(16, x0 * x0)
                add(17, x0 * x1)
                add(18, x1 * x1)
                add(19, force * x0)
                add(20, force * x1)
                add(21, force * force)
        for i in range(22):
            totals[i] += parts[i]
        return carry

    def step(tau, carry):
        for s in (1, 0):
            for p in range(2):
                far_off = distance[s][p]
                k = tau - far_off

                @pl.when((k >= 0) & (k < pieces))
                def _():
                    @pl.when(far_off > 0)
                    def _():
                        hop(s, p, k).wait_recv()

                    @pl.when(far_off < n_real - 1)
                    def _():
                        hop(s, p, k).start()

                    edge_hop(s, p, k).start()

        done = tau - (n_real - 1) - LAG

        @pl.when(done == 0)
        def _():
            load_copy.wait()
            for p in range(2):
                root_hop(p).wait_recv()

        @pl.when(done >= 0)
        def _():
            for s in range(2):
                for p in range(2):
                    edge_hop(s, p, done).wait_recv()
            lax.fori_loop(done * (ROWS // 8), (done + 1) * (ROWS // 8), mix, 0)
            per = ROWS // width
            lax.fori_loop(jnp.maximum(done * per - 1, 1), (done + 1) * per - 1, work, 0)

        return carry

    lax.fori_loop(0, pieces + n_real - 1 + LAG, step, 0)

    for s in range(2):
        for p in range(2):
            mixed[s, p, 0:PAD, :] = mixed[s, p, circ : circ + PAD, :]
            mixed[s, p, circ + PAD : circ + 2 * PAD, :] = mixed[s, p, PAD : 2 * PAD, :]
    lax.fori_loop(0, 2, lambda i, c: work((1 - i) * (sectors - 1), c), 0)

    lane = lax.broadcasted_iota(jnp.int32, (8, LANES), 1)
    packed = jnp.zeros((8, LANES), F32)
    for g in range(3):
        v = jnp.sum(totals[8 * g : 8 * g + 8], axis=1)
        v = v + pltpu.roll(v, 64, 1)
        v = v + pltpu.roll(v, 32, 1)
        packed = jnp.where((lane >= 32 * g) & (lane < 32 * g + 32), v, packed)

    def near_hop(i):
        return pltpu.make_async_remote_copy(
            src_ref=near.at[my_near],
            dst_ref=near.at[my_near],
            send_sem=near_send.at[i],
            recv_sem=near_recv.at[i],
            device_id={"span": near_peer(i)},
            device_id_type=MESH,
        )

    def far_hop(i):
        return pltpu.make_async_remote_copy(
            src_ref=far.at[my_far],
            dst_ref=far.at[my_far],
            send_sem=far_send.at[i],
            recv_sem=far_recv.at[i],
            device_id={"span": far_peer(i)},
            device_id_type=MESH,
        )

    near[my_near] = packed
    for i in range(1, n_near):
        near_hop(i).start()
    for i in range(1, n_near):
        near_hop(i).wait_recv()
    far[my_far] = jnp.sum(near[...], axis=0)
    for i in range(1, n_far):
        far_hop(i).start()
    for i in range(1, n_far):
        far_hop(i).wait_recv()

    group = lax.broadcasted_iota(jnp.int32, (1, LANES), 1) // 32
    rows = [far[:, r, :] for r in range(8)]

    def one(x, g):
        return jnp.sum(jnp.where(group == g, x, 0.0), axis=1, keepdims=True)

    def total(x):
        x = jnp.sum(x, axis=0, keepdims=True)
        return jnp.where(group == 0, one(x, 0), one(x, 1)) / cells

    def shared(x):
        return one(jnp.sum(x, axis=0, keepdims=True), 2) / cells

    swapped = picks[0] == last
    r00, r01, r11 = jnp.where(swapped, rows[2], rows[0]), rows[1], jnp.where(swapped, rows[0], rows[2])
    f0, f1 = jnp.where(swapped, rows[4], rows[3]), jnp.where(swapped, rows[3], rows[4])
    norm0 = shared(r00)
    along = shared(r01) / norm0
    rest = r11 - 2.0 * along * r01 + along * along * r00
    norm1 = shared(rest)
    inv0, inv1 = 1.0 / jnp.sqrt(norm0), 1.0 / jnp.sqrt(norm1)
    a00 = total(r00) * inv0 * inv0
    a01 = total(r01 - along * r00) * inv0 * inv1
    a11 = total(rest) * inv1 * inv1
    b0, b1 = shared(f0) * inv0, shared(f1 - along * f0) * inv1
    det = a00 * a11 - a01 * a01
    c0, c1 = (a11 * b0 - a01 * b1) / det, (a00 * b1 - a01 * b0) / det
    second = c1 * inv1
    first = c0 * inv0 - along * second
    g0, g1 = jnp.where(swapped, second, first), jnp.where(swapped, first, second)
    power = jnp.where(group == 0, pltpu.roll(rows[5], 64, 1), pltpu.roll(rows[5], 96, 1))
    square = total(
        power
        - 2.0 * (g0 * rows[3] + g1 * rows[4])
        + (g0 * g0 * rows[5] + 2.0 * g0 * g1 * rows[6] + g1 * g1 * rows[7])
    )
    spot = lax.broadcasted_iota(jnp.int32, (1, LANES), 1)

    def scalar(x, t):
        return jnp.sum(jnp.where(spot == 32 * t, x, 0.0))

    for t in range(2):
        red[t, 0, 0] = scalar(a00, t)
        red[t, 0, 1] = scalar(a01, t)
        red[t, 1, 0] = scalar(a01, t)
        red[t, 1, 1] = scalar(a11, t)
        nrm[t] = scalar(square, t)

    scale = [[jnp.sum(jnp.where(spot == 32 * t, g, 0.0), axis=1, keepdims=True) for g in (g0, g1)] for t in range(2)]
    blocks = 8
    tall = circ // blocks

    def out_copy(t, b):
        rows = pl.ds(pl.multiple_of(b * tall, tall), tall)
        return pltpu.make_async_copy(image.at[t, 0, :, rows], res.at[t, :, rows], local_sem.at[4 + t])

    def finish(b, carry):
        def block(i, c):
            rows = pl.ds(pl.multiple_of(b * tall + i * 8, 8), 8)
            for p in range(planes):
                force = load[p, rows, :]
                for t in range(2):
                    image[t, 0, p, rows, :] = force - (
                        scale[t][0] * image[t, 0, p, rows, :] + scale[t][1] * image[t, 1, p, rows, :]
                    )
            return c

        lax.fori_loop(0, tall // 8, block, 0)
        for t in range(2):
            out_copy(t, b).start()
        return carry

    lax.fori_loop(0, blocks, finish, 0)

    for p in range(2):
        root_hop(p).wait_send()
    for i in range(1, n_near):
        near_hop(i).wait_send()
    for i in range(1, n_far):
        far_hop(i).wait_send()

    def whole(s, p, sem):
        return pltpu.make_async_copy(field.at[s, p], field.at[s, p], sem)

    for s in range(2):
        for p in range(2):
            whole(s, p, edge_send.at[s, p]).wait()

            @pl.when(distance[s][p] < n_real - 1)
            def _():
                whole(s, p, send_sem.at[s, p]).wait()

    for t in range(2):
        pltpu.make_async_copy(image.at[t, 0], res.at[t], local_sem.at[4 + t]).wait()


def shards(snapshots, load, base_modulus, mistune, material_ids, realization_map, picks):
    n_span, n_real = lax.axis_size("span"), lax.axis_size("real")
    held, planes, circ, axial = snapshots.shape
    n_near = 8 if n_span % 8 == 0 else 2
    n_far = n_span // n_near
    pieces = circ // ROWS
    vmem = lambda *shape: pltpu.VMEM(shape, F32)
    dma = lambda *shape: pltpu.SemaphoreType.DMA(shape)

    def run(owner):
        return pl.pallas_call(
            functools.partial(kernel, owner),
            out_shape=(
                jax.ShapeDtypeStruct((2, 2, 2), F32),
                jax.ShapeDtypeStruct((2, planes, circ, axial), F32),
                jax.ShapeDtypeStruct((2,), F32),
            ),
            in_specs=[pl.BlockSpec(memory_space=pltpu.SMEM)] * 4 + [pl.BlockSpec(memory_space=pl.ANY)] * 3,
            out_specs=(
                pl.BlockSpec(memory_space=pltpu.SMEM),
                pl.BlockSpec(memory_space=pl.ANY),
                pl.BlockSpec(memory_space=pltpu.SMEM),
            ),
            scratch_shapes=[
                vmem(2, planes, circ, axial),
                vmem(2, 2, circ, axial),
                vmem(held, planes, circ, axial),
                vmem(planes, circ, axial),
                vmem(planes, circ, axial),
                vmem(2, circ, axial),
                vmem(2, planes, circ + 2 * PAD, axial),
                vmem(2, 2, planes, circ, axial),
                vmem(2, circ + 2 * PAD, LANES),
                vmem(2, 2, circ, LANES),
                vmem(24, 8, LANES),
                vmem(n_near, 8, LANES),
                vmem(n_far, 8, LANES),
                dma(6),
                dma(2, 2),
                dma(2, 2, pieces),
                dma(2, 2),
                dma(2, 2, pieces),
                dma(2),
                dma(2),
                dma(n_near),
                dma(n_near),
                dma(n_far),
                dma(n_far),
            ],
            compiler_params=pltpu.CompilerParams(
                collective_id=owner, has_side_effects=True, vmem_limit_bytes=40 * 2**20
            ),
        )(picks, mistune, material_ids, realization_map, snapshots, load, base_modulus)

    other = jnp.minimum(picks[0], picks[1])
    return lax.switch(
        lax.div(other, jnp.int32(held)), [lambda owner=owner: run(owner) for owner in range(n_real)]
    )


def solution(mesh):
    return jax.shard_map(
        shards,
        mesh=mesh,
        in_specs=(
            P("real", "span", None, None),
            P("span", None, None),
            P("span", None, None),
            P(),
            P(),
            P("real"),
            P(),
        ),
        out_specs=(P("real", None, None), P("real", "span", None, None), P("real")),
        check_vma=False,
    )
```

```python
import functools

import jax
import jax.numpy as jnp
from jax import lax
from jax.experimental import pallas as pl
from jax.experimental.pallas import tpu as pltpu
from jax.sharding import PartitionSpec as P

MESH = pl.DeviceIdType.MESH
SHIFT = 0.5
ROWS = 32
DEPTH = 2
LAG = 2
PAD = 8
LANES = 128
F32 = jnp.float32


def gather_kernel(
    picks_in, mistune_in, ids_in, slots_in, snaps, load_in, base_in,
    image, load, far, order,
    picks, mistune, ids, slots,
    field, edge, both, own, sent, got, root, root_edge, mixed, factor, pair, totals, near,
    small_sem, local_sem, send_sem, recv_sem, sent_sem, got_sem, edge_send, edge_recv, root_send, root_recv,
    near_send, near_recv, far_send, far_recv,
):
    n_span, n_real = lax.axis_size("span"), lax.axis_size("real")
    span, real = lax.axis_index("span"), lax.axis_index("real")
    held, planes, circ, axial = snaps.shape
    sectors = ids_in.shape[1]
    width = circ // sectors
    pieces = circ // ROWS
    last = held * n_real - 1
    slots_sent = pieces + (n_real - 2) * DEPTH
    n_near, n_far = near.shape[0], far.shape[0]

    before, after = lax.rem(span + n_span - 1, n_span), lax.rem(span + 1, n_span)
    below, above = lax.rem(real + n_real - 1, n_real), lax.rem(real + 1, n_real)
    my_far, my_near = lax.div(span, n_near), lax.rem(span, n_near)

    def near_peer(i):
        return my_far * n_near + lax.rem(my_near + i, n_near)

    def far_peer(i):
        return lax.rem(my_far + i, n_far) * n_near + my_near

    barrier = pltpu.get_barrier_semaphore()
    greeted = 0
    for where in [{"real": below}, {"real": above}, {"span": before}, {"span": after}]:
        pl.semaphore_signal(barrier, inc=1, device_id=where, device_id_type=MESH)
        greeted += 1
    for i in range(1, n_near):
        pl.semaphore_signal(barrier, inc=1, device_id={"span": near_peer(i)}, device_id_type=MESH)
        greeted += 1
    for i in range(1, n_far):
        pl.semaphore_signal(barrier, inc=1, device_id={"span": far_peer(i)}, device_id_type=MESH)
        greeted += 1

    smalls = [
        pltpu.make_async_copy(src, dst, small_sem.at[i])
        for i, (src, dst) in enumerate(((picks_in, picks), (mistune_in, mistune), (ids_in, ids), (slots_in, slots)))
    ]
    base_copy = pltpu.make_async_copy(base_in, root, local_sem.at[0])
    load_copy = pltpu.make_async_copy(load_in, load, local_sem.at[1])
    last_copy = pltpu.make_async_copy(snaps.at[held - 1], field.at[1], local_sem.at[2])
    both_copy = pltpu.make_async_copy(snaps, both, local_sem.at[3])
    for copy in smalls:
        copy.start()
    base_copy.start()
    both_copy.start()

    @pl.when(real == n_real - 1)
    def _():
        last_copy.start()

    load_copy.start()
    for copy in smalls:
        copy.wait()
    other = jnp.minimum(picks[0], picks[1])
    order[...] = jnp.full(order.shape, jnp.where(picks[0] == last, 1.0, 0.0), F32)

    def fill(j, carry):
        for t in range(2):
            value = mistune[ids[slots[t], j]]
            factor[t, pl.ds(PAD + j * width, width), :] = jnp.full((width, LANES), value, F32)
        return carry

    lax.fori_loop(0, sectors, fill, 0)
    for t in range(2):
        factor[t, 0:PAD, :] = factor[t, circ : circ + PAD, :]
        factor[t, circ + PAD : circ + 2 * PAD, :] = factor[t, PAD : 2 * PAD, :]
        here = factor[t, PAD : circ + PAD, :]
        for side, shift in ((0, -1), (1, 1)):
            pair[t, side] = jnp.sqrt(here * factor[t, PAD + shift : circ + PAD + shift, :])
    totals[...] = jnp.zeros_like(totals)

    base_copy.wait()
    both_copy.wait()
    chosen = lax.rem(other, held)

    def take_root(i, carry):
        rows = pl.ds(pl.multiple_of(i * 16, 16), 16)
        for p in range(planes):
            root[p, rows, :] = jnp.sqrt(root[p, rows, :])
            own[p, rows, :] = jnp.where(chosen == 0, both[0, p, rows, :], both[held - 1, p, rows, :])
        return carry

    lax.fori_loop(0, circ // 16, take_root, 0)

    @pl.when(real == n_real - 1)
    def _():
        last_copy.wait()

    pl.semaphore_wait(barrier, greeted)

    def root_hop(p):
        return pltpu.make_async_remote_copy(
            src_ref=root.at[p],
            dst_ref=root_edge.at[1 - p],
            send_sem=root_send.at[p],
            recv_sem=root_recv.at[1 - p],
            device_id={"span": before if p == 0 else after},
            device_id_type=MESH,
        )

    for p in range(2):
        root_hop(p).start()

    def rows_of(k):
        return pl.ds(pl.multiple_of(k * ROWS, ROWS), ROWS)

    def along(p):
        return {"real": above if p == 0 else below}

    def hop(p, k):
        return pltpu.make_async_remote_copy(
            src_ref=field.at[1, p, rows_of(k)],
            dst_ref=field.at[1, p, rows_of(k)],
            send_sem=send_sem.at[p],
            recv_sem=recv_sem.at[p, k],
            device_id=along(p),
            device_id_type=MESH,
        )

    def pass_on(p, k):
        return pltpu.make_async_remote_copy(
            src_ref=sent.at[p, rows_of(k)],
            dst_ref=got.at[p, rows_of(k)],
            send_sem=sent_sem.at[p],
            recv_sem=got_sem.at[p, k],
            device_id=along(p),
            device_id_type=MESH,
        )

    def edge_hop(s, p, k):
        return pltpu.make_async_remote_copy(
            src_ref=field.at[s, p, rows_of(k)],
            dst_ref=edge.at[s, 1 - p, rows_of(k)],
            send_sem=edge_send.at[s, p],
            recv_sem=edge_recv.at[s, 1 - p, k],
            device_id={"span": before if p == 0 else after},
            device_id_type=MESH,
        )

    distance = (real + 1) % n_real, n_real - 1 - real
    owner = lax.div(other, held)
    from_owner = (lax.rem(real + n_real - owner, n_real), lax.rem(owner + n_real - real, n_real))

    low = jnp.where(span > 0, 0.5, 0.0).astype(F32)
    high = jnp.where(span < n_span - 1, 0.5, 0.0).astype(F32)
    column = lax.broadcasted_iota(jnp.int32, (8, axial), 1)
    not_first, not_last = column > 0, column < axial - 1

    def mix(k, carry):
        start = pl.multiple_of(k * 8, 8)
        rows = pl.ds(start, 8)
        q0, q1, ql, qh = root[0, rows, :], root[1, rows, :], root_edge[0, rows, :], root_edge[1, rows, :]
        for s in range(2):
            w0, w1 = q0 * field[s, 0, rows, :], q1 * field[s, 1, rows, :]
            wl, wh = ql * edge[s, 0, rows, :], qh * edge[s, 1, rows, :]
            for p, across in ((0, w0 + (low * wl + 0.5 * w1)), (1, w1 + (high * wh + 0.5 * w0))):
                left = jnp.where(not_first, pltpu.roll(across, 1, 1), 0.0)
                right = jnp.where(not_last, pltpu.roll(across, axial - 1, 1), 0.0)
                mixed[s, p, pl.ds(start + PAD, 8), :] = across + 0.5 * (left + right)
        return carry

    def fold(x):
        return x[:, :LANES] + x[:, LANES:]

    def work(j, carry):
        parts = [None] * 22

        def add(i, x):
            x = fold(x)
            parts[i] = x if parts[i] is None else parts[i] + x

        for h in range(width // 8):
            start = pl.multiple_of(j * width + h * 8, 8)
            rows = pl.ds(start, 8)
            wide = lambda x: jnp.concatenate([x] * (axial // LANES), axis=1)
            fac = [wide(factor[t, pl.ds(start + PAD, 8), :]) for t in range(2)]
            prev = [wide(pair[t, 0, rows, :]) for t in range(2)]
            succ = [wide(pair[t, 1, rows, :]) for t in range(2)]
            for p in range(planes):
                q, force = root[p, rows, :], load[p, rows, :]
                x0, x1 = field[0, p, rows, :], field[1, p, rows, :]
                images = [[None, None], [None, None]]
                for s, x in ((0, x0), (1, x1)):
                    tall = mixed[s, p, pl.ds(start + PAD - 8, 24), :]
                    up, centre, down = tall[7:15], tall[8:16], tall[9:17]
                    inner = (16.0 + SHIFT) * (q * x) - 2.0 * centre
                    for t in range(2):
                        im = q * (fac[t] * inner - (prev[t] * up + succ[t] * down))
                        image[t, s, p, rows, :] = im
                        images[t][s] = im
                for t in range(2):
                    i0, i1 = images[t]
                    add(8 * t + 0, x0 * i0)
                    add(8 * t + 1, x0 * i1)
                    add(8 * t + 2, x1 * i1)
                    add(8 * t + 3, force * i0)
                    add(8 * t + 4, force * i1)
                    add(8 * t + 5, i0 * i0)
                    add(8 * t + 6, i0 * i1)
                    add(8 * t + 7, i1 * i1)
                add(16, x0 * x0)
                add(17, x0 * x1)
                add(18, x1 * x1)
                add(19, force * x0)
                add(20, force * x1)
                add(21, force * force)
        for i in range(22):
            totals[i] += parts[i]
        return carry

    def step(tau, carry):
        for p in range(2):
            far_off = distance[p]
            k = tau - DEPTH * far_off

            @pl.when((k >= 0) & (k < pieces))
            def _():
                @pl.when(far_off > 0)
                def _():
                    hop(p, k).wait_recv()

                @pl.when(far_off < n_real - 1)
                def _():
                    hop(p, k).start()

                edge_hop(1, p, k).start()

        for p in range(2):
            @pl.when(tau < DEPTH)
            def _():
                sent[p, rows_of(tau), :] = own[p, rows_of(tau), :]

            @pl.when((tau >= DEPTH) & (tau < slots_sent + DEPTH))
            def _():
                pass_on(p, tau - DEPTH).wait_recv()

            @pl.when((tau >= DEPTH) & (tau < slots_sent))
            def _():
                mine = own[p, rows_of(jnp.minimum(tau, pieces - 1)), :]
                sent[p, rows_of(tau), :] = jnp.where(from_owner[p] == 0, mine, got[p, rows_of(tau - DEPTH), :])

            @pl.when(tau < slots_sent)
            def _():
                pass_on(p, tau).start()

            @pl.when((tau >= (n_real - 1) * DEPTH) & (tau < slots_sent + DEPTH))
            def _():
                k = tau - (n_real - 1) * DEPTH
                piece = own[p, rows_of(k), :]
                for d in range(1, n_real):
                    piece = jnp.where(from_owner[p] == d, got[p, rows_of(k + (d - 1) * DEPTH), :], piece)
                field[0, p, rows_of(k), :] = piece
                edge_hop(0, p, k).start()

        done = tau - (n_real - 1) * DEPTH - LAG

        @pl.when(done == 0)
        def _():
            load_copy.wait()
            for p in range(2):
                root_hop(p).wait_recv()

        @pl.when(done >= 0)
        def _():
            for s in range(2):
                for p in range(2):
                    edge_hop(s, p, done).wait_recv()
            lax.fori_loop(done * (ROWS // 8), (done + 1) * (ROWS // 8), mix, 0)
            per = ROWS // width
            lax.fori_loop(jnp.maximum(done * per - 1, 1), (done + 1) * per - 1, work, 0)

        return carry

    lax.fori_loop(0, pieces + (n_real - 1) * DEPTH + LAG, step, 0)

    for s in range(2):
        for p in range(2):
            mixed[s, p, 0:PAD, :] = mixed[s, p, circ : circ + PAD, :]
            mixed[s, p, circ + PAD : circ + 2 * PAD, :] = mixed[s, p, PAD : 2 * PAD, :]
    lax.fori_loop(0, 2, lambda i, c: work((1 - i) * (sectors - 1), c), 0)

    lane = lax.broadcasted_iota(jnp.int32, (8, LANES), 1)
    packed = jnp.zeros((8, LANES), F32)
    for g in range(3):
        v = jnp.sum(totals[8 * g : 8 * g + 8], axis=1)
        v = v + pltpu.roll(v, 64, 1)
        v = v + pltpu.roll(v, 32, 1)
        packed = jnp.where((lane >= 32 * g) & (lane < 32 * g + 32), v, packed)

    def near_hop(i):
        return pltpu.make_async_remote_copy(
            src_ref=near.at[my_near],
            dst_ref=near.at[my_near],
            send_sem=near_send.at[i],
            recv_sem=near_recv.at[i],
            device_id={"span": near_peer(i)},
            device_id_type=MESH,
        )

    def far_hop(i):
        return pltpu.make_async_remote_copy(
            src_ref=far.at[my_far],
            dst_ref=far.at[my_far],
            send_sem=far_send.at[i],
            recv_sem=far_recv.at[i],
            device_id={"span": far_peer(i)},
            device_id_type=MESH,
        )

    near[my_near] = packed
    for i in range(1, n_near):
        near_hop(i).start()
    for i in range(1, n_near):
        near_hop(i).wait_recv()
    far[my_far] = jnp.sum(near[...], axis=0)
    for i in range(1, n_far):
        far_hop(i).start()
    for i in range(1, n_far):
        far_hop(i).wait_recv()

    for p in range(2):
        root_hop(p).wait_send()
    for i in range(1, n_near):
        near_hop(i).wait_send()
    for i in range(1, n_far):
        far_hop(i).wait_send()

    def whole(s, p, sem):
        return pltpu.make_async_copy(field.at[s, p], field.at[s, p], sem)

    for p in range(2):
        for s in range(2):
            whole(s, p, edge_send.at[s, p]).wait()

        @pl.when(distance[p] < n_real - 1)
        def _():
            whole(1, p, send_sem.at[p]).wait()

        pltpu.make_async_copy(sent.at[p], sent.at[p], sent_sem.at[p]).wait()


def finish_kernel(image, load, far, order, red, res, nrm, out, sems, *, cells):
    planes, circ, axial = load.shape
    group = lax.broadcasted_iota(jnp.int32, (1, LANES), 1) // 32
    rows = [far[:, r, :] for r in range(8)]

    def one(x, g):
        return jnp.sum(jnp.where(group == g, x, 0.0), axis=1, keepdims=True)

    def total(x):
        x = jnp.sum(x, axis=0, keepdims=True)
        return jnp.where(group == 0, one(x, 0), one(x, 1)) / cells

    def shared(x):
        return one(jnp.sum(x, axis=0, keepdims=True), 2) / cells

    swapped = order[0:1, :] > 0.5
    r00, r01, r11 = jnp.where(swapped, rows[2], rows[0]), rows[1], jnp.where(swapped, rows[0], rows[2])
    f0, f1 = jnp.where(swapped, rows[4], rows[3]), jnp.where(swapped, rows[3], rows[4])
    norm0 = shared(r00)
    along = shared(r01) / norm0
    rest = r11 - 2.0 * along * r01 + along * along * r00
    norm1 = shared(rest)
    inv0, inv1 = 1.0 / jnp.sqrt(norm0), 1.0 / jnp.sqrt(norm1)
    a00 = total(r00) * inv0 * inv0
    a01 = total(r01 - along * r00) * inv0 * inv1
    a11 = total(rest) * inv1 * inv1
    b0, b1 = shared(f0) * inv0, shared(f1 - along * f0) * inv1
    det = a00 * a11 - a01 * a01
    c0, c1 = (a11 * b0 - a01 * b1) / det, (a00 * b1 - a01 * b0) / det
    second = c1 * inv1
    first = c0 * inv0 - along * second
    g0, g1 = jnp.where(swapped, second, first), jnp.where(swapped, first, second)
    power = jnp.where(group == 0, pltpu.roll(rows[5], 64, 1), pltpu.roll(rows[5], 96, 1))
    square = total(
        power
        - 2.0 * (g0 * rows[3] + g1 * rows[4])
        + (g0 * g0 * rows[5] + 2.0 * g0 * g1 * rows[6] + g1 * g1 * rows[7])
    )
    spot = lax.broadcasted_iota(jnp.int32, (1, LANES), 1)

    scale = [[jnp.sum(jnp.where(spot == 32 * t, g, 0.0), axis=1, keepdims=True) for g in (g0, g1)] for t in range(2)]
    blocks = 8
    tall = circ // blocks

    def out_copy(t, b):
        rows = pl.ds(pl.multiple_of(b * tall, tall), tall)
        return pltpu.make_async_copy(out.at[t, :, rows], res.at[t, :, rows], sems.at[t])

    def finish(b, carry):
        def block(i, c):
            rows = pl.ds(pl.multiple_of(b * tall + i * 8, 8), 8)
            for p in range(planes):
                force = load[p, rows, :]
                for t in range(2):
                    out[t, p, rows, :] = force - (
                        scale[t][0] * image[t, 0, p, rows, :] + scale[t][1] * image[t, 1, p, rows, :]
                    )
            return c

        lax.fori_loop(0, tall // 8, block, 0)
        for t in range(2):
            out_copy(t, b).start()
        return carry

    lax.fori_loop(0, blocks, finish, 0)

    def scalar(x, t):
        return jnp.sum(jnp.where(spot == 32 * t, x, 0.0))

    for t in range(2):
        red[t, 0, 0] = scalar(a00, t)
        red[t, 0, 1] = scalar(a01, t)
        red[t, 1, 0] = scalar(a01, t)
        red[t, 1, 1] = scalar(a11, t)
        nrm[t] = scalar(square, t)

    for t in range(2):
        pltpu.make_async_copy(out.at[t], res.at[t], sems.at[t]).wait()


def shards(snapshots, load, base_modulus, mistune, material_ids, realization_map, picks):
    n_span, n_real = lax.axis_size("span"), lax.axis_size("real")
    held, planes, circ, axial = snapshots.shape
    n_near = 8 if n_span % 8 == 0 else 2
    n_far = n_span // n_near
    pieces = circ // ROWS
    vmem = lambda *shape: pltpu.VMEM(shape, F32)
    dma = lambda *shape: pltpu.SemaphoreType.DMA(shape)

    kept = pieces + (n_real - 2) * DEPTH
    whole = lambda space, count: [pl.BlockSpec(memory_space=space)] * count
    sums = pl.pallas_call(
        gather_kernel,
        out_shape=(
            vmem(2, 2, planes, circ, axial),
            vmem(planes, circ, axial),
            vmem(n_far, 8, LANES),
            vmem(8, LANES),
        ),
        in_specs=whole(pltpu.HBM, 7),
        out_specs=tuple(whole(pltpu.VMEM, 4)),
        scratch_shapes=[
            pltpu.SMEM(picks.shape, jnp.int32),
            pltpu.SMEM(mistune.shape, F32),
            pltpu.SMEM(material_ids.shape, jnp.int32),
            pltpu.SMEM(realization_map.shape, jnp.int32),
            vmem(2, planes, circ, axial),
            vmem(2, 2, circ, axial),
            vmem(held, planes, circ, axial),
            vmem(planes, circ, axial),
            vmem(planes, kept * ROWS, axial),
            vmem(planes, kept * ROWS, axial),
            vmem(planes, circ, axial),
            vmem(2, circ, axial),
            vmem(2, planes, circ + 2 * PAD, axial),
            vmem(2, circ + 2 * PAD, LANES),
            vmem(2, 2, circ, LANES),
            vmem(24, 8, LANES),
            vmem(n_near, 8, LANES),
            dma(4),
            dma(4),
            dma(2),
            dma(2, pieces),
            dma(2),
            dma(2, kept),
            dma(2, 2),
            dma(2, 2, pieces),
            dma(2),
            dma(2),
            dma(n_near),
            dma(n_near),
            dma(n_far),
            dma(n_far),
        ],
        compiler_params=pltpu.CompilerParams(
            collective_id=0, has_side_effects=True, vmem_limit_bytes=58720256
        ),
    )(picks, mistune, material_ids, realization_map, snapshots, load, base_modulus)
    return pl.pallas_call(
        functools.partial(finish_kernel, cells=float(planes * n_span * circ * axial)),
        out_shape=(
            jax.ShapeDtypeStruct((2, 2, 2), F32),
            jax.ShapeDtypeStruct((2, planes, circ, axial), F32),
            jax.ShapeDtypeStruct((2,), F32),
        ),
        in_specs=whole(pltpu.VMEM, 4),
        out_specs=(
            pl.BlockSpec(memory_space=pltpu.SMEM),
            pl.BlockSpec(memory_space=pltpu.HBM),
            pl.BlockSpec(memory_space=pltpu.SMEM),
        ),
        scratch_shapes=[vmem(2, planes, circ, axial), dma(2)],
        compiler_params=pltpu.CompilerParams(vmem_limit_bytes=40 * 2**20),
    )(*sums)


def solution(mesh):
    return jax.shard_map(
        shards,
        mesh=mesh,
        in_specs=(
            P("real", "span", None, None),
            P("span", None, None),
            P("span", None, None),
            P(),
            P(),
            P("real"),
            P(),
        ),
        out_specs=(P("real", None, None), P("real", "span", None, None), P("real")),
        check_vma=False,
    )
```

```python
import functools

import jax
import jax.numpy as jnp
from jax import lax
from jax.experimental import pallas as pl
from jax.experimental.pallas import tpu as pltpu
from jax.sharding import PartitionSpec as P

MESH = pl.DeviceIdType.MESH
SHIFT = 0.5
ROWS = 32
DEPTH = 3
LAG = 1
PAD = 8
LANES = 128
F32 = jnp.float32


def gather_kernel(
    picks_in, mistune_in, ids_in, slots_in, snaps, load_in, base_in,
    image, load, far, order,
    picks, mistune, ids, slots,
    field, edge, both, own, sent, got, root, root_edge, mixed, factor, pair, totals, mate, hub,
    small_sem, local_sem, send_sem, recv_sem, sent_sem, got_sem, edge_send, edge_recv, root_send, root_recv,
    mate_send, mate_recv, hub_send, hub_recv,
):
    n_span, n_real = lax.axis_size("span"), lax.axis_size("real")
    span, real = lax.axis_index("span"), lax.axis_index("real")
    held, planes, circ, axial = snaps.shape
    sectors = ids_in.shape[1]
    width = circ // sectors
    pieces = circ // ROWS
    last = held * n_real - 1
    slots_sent = pieces + (n_real - 2) * DEPTH
    before, after = lax.rem(span + n_span - 1, n_span), lax.rem(span + 1, n_span)
    below, above = lax.rem(real + n_real - 1, n_real), lax.rem(real + 1, n_real)
    core, chip, chips = lax.rem(span, 2), lax.div(span, 2), n_span // 2
    outer, inner = core, 1 - core
    hubs = chips // 2

    def partner(step):
        return 2 * lax.rem(chip + core * hubs + step, chips) + core

    barrier = pltpu.get_barrier_semaphore()
    for where in [{"real": below}, {"real": above}, {"span": before}, {"span": after}]:
        pl.semaphore_signal(barrier, inc=1, device_id=where, device_id_type=MESH)
    for i in range(hubs):
        source = 2 * lax.rem(chip + chips - (core * hubs + i), chips) + core

        @pl.when(core * hubs + i > 0)
        def _():
            pl.semaphore_signal(barrier, inc=1, device_id={"span": source}, device_id_type=MESH)

    smalls = [
        pltpu.make_async_copy(src, dst, small_sem.at[i])
        for i, (src, dst) in enumerate(((picks_in, picks), (mistune_in, mistune), (ids_in, ids), (slots_in, slots)))
    ]
    base_copy = pltpu.make_async_copy(base_in, root, local_sem.at[0])
    load_copy = pltpu.make_async_copy(load_in, load, local_sem.at[1])
    last_copy = pltpu.make_async_copy(snaps.at[held - 1], field.at[1], local_sem.at[2])
    both_copy = pltpu.make_async_copy(snaps, both, local_sem.at[3])
    for copy in smalls:
        copy.start()
    base_copy.start()
    both_copy.start()

    @pl.when(real == n_real - 1)
    def _():
        last_copy.start()

    load_copy.start()
    for copy in smalls:
        copy.wait()
    other = jnp.minimum(picks[0], picks[1])
    order[...] = jnp.full(order.shape, jnp.where(picks[0] == last, 1.0, 0.0), F32)

    base_copy.wait()
    both_copy.wait()
    chosen = lax.rem(other, held)

    def take_root(i, carry):
        rows = pl.ds(pl.multiple_of(i * 16, 16), 16)
        for p in range(planes):
            root[p, rows, :] = jnp.sqrt(root[p, rows, :])
            own[p, rows, :] = jnp.where(chosen == 0, both[0, p, rows, :], both[held - 1, p, rows, :])
        return carry

    lax.fori_loop(0, circ // 16, take_root, 0)

    @pl.when(real == n_real - 1)
    def _():
        last_copy.wait()

    pl.semaphore_wait(barrier, 4 + hubs - 1 + core)

    def root_hop(p):
        return pltpu.make_async_remote_copy(
            src_ref=root.at[p],
            dst_ref=root_edge.at[1 - p],
            send_sem=root_send.at[p],
            recv_sem=root_recv.at[1 - p],
            device_id={"span": before if p == 0 else after},
            device_id_type=MESH,
        )

    for p in range(2):
        root_hop(p).start()

    def rows_of(k):
        return pl.ds(pl.multiple_of(k * ROWS, ROWS), ROWS)

    half = pieces // 2

    def plane_of(k):
        return jnp.where(k < half, outer, inner)

    def place(p, k):
        return rows_of(p * half + lax.rem(k, half))

    def prepare():
        def fill(j, carry):
            for t in range(2):
                value = mistune[ids[slots[t], j]]
                factor[t, pl.ds(PAD + j * width, width), :] = jnp.full((width, LANES), value, F32)
            return carry

        lax.fori_loop(0, sectors, fill, 0)
        for t in range(2):
            factor[t, 0:PAD, :] = factor[t, circ : circ + PAD, :]
            factor[t, circ + PAD : circ + 2 * PAD, :] = factor[t, PAD : 2 * PAD, :]
            here = factor[t, PAD : circ + PAD, :]
            for side, shift in ((0, -1), (1, 1)):
                pair[t, side] = jnp.sqrt(here * factor[t, PAD + shift : circ + PAD + shift, :])
        totals[...] = jnp.zeros_like(totals)

    def along(p):
        return {"real": above if p == 0 else below}

    def hop(p, k):
        return pltpu.make_async_remote_copy(
            src_ref=field.at[1, plane_of(k), place(p, k)],
            dst_ref=field.at[1, plane_of(k), place(p, k)],
            send_sem=send_sem.at[p],
            recv_sem=recv_sem.at[p, k],
            device_id=along(p),
            device_id_type=MESH,
        )

    def pass_on(p, k):
        return pltpu.make_async_remote_copy(
            src_ref=sent.at[p, rows_of(k)],
            dst_ref=got.at[p, rows_of(k)],
            send_sem=sent_sem.at[p],
            recv_sem=got_sem.at[p, k],
            device_id=along(p),
            device_id_type=MESH,
        )

    def edge_hop(s, p, k):
        plane = plane_of(k)
        return pltpu.make_async_remote_copy(
            src_ref=field.at[s, plane, place(p, k)],
            dst_ref=edge.at[s, 1 - plane, place(p, k)],
            send_sem=edge_send.at[s, p],
            recv_sem=edge_recv.at[s, p, k],
            device_id={"span": jnp.where(plane == 0, before, after)},
            device_id_type=MESH,
        )

    def edge_arrives(s, p, k):
        here = edge.at[s, plane_of(k), place(p, k)]
        pltpu.make_async_copy(here, here, edge_recv.at[s, p, k]).wait()

    distance = (real + 1) % n_real, n_real - 1 - real
    owner = lax.div(other, held)
    from_owner = (lax.rem(real + n_real - owner, n_real), lax.rem(owner + n_real - real, n_real))

    low = jnp.where(span > 0, 0.5, 0.0).astype(F32)
    high = jnp.where(span < n_span - 1, 0.5, 0.0).astype(F32)
    column = lax.broadcasted_iota(jnp.int32, (8, axial), 1)
    not_first, not_last = column > 0, column < axial - 1

    def mix(k, carry):
        for p in range(2):
            mix_rows(pl.multiple_of(p * (circ // 2) + k * 8, 8))
        return carry

    def mix_rows(start):
        rows = pl.ds(start, 8)
        q0, q1, ql, qh = root[0, rows, :], root[1, rows, :], root_edge[0, rows, :], root_edge[1, rows, :]
        for s in range(2):
            w0, w1 = q0 * field[s, 0, rows, :], q1 * field[s, 1, rows, :]
            wl, wh = ql * edge[s, 0, rows, :], qh * edge[s, 1, rows, :]
            for p, across in ((0, w0 + (low * wl + 0.5 * w1)), (1, w1 + (high * wh + 0.5 * w0))):
                left = jnp.where(not_first, pltpu.roll(across, 1, 1), 0.0)
                right = jnp.where(not_last, pltpu.roll(across, axial - 1, 1), 0.0)
                mixed[s, p, pl.ds(start + PAD, 8), :] = across + 0.5 * (left + right)

    def fold(x):
        return x[:, :LANES] + x[:, LANES:]

    def work(j, carry):
        parts = [None] * 22

        def add(i, x):
            x = fold(x)
            parts[i] = x if parts[i] is None else parts[i] + x

        for h in range(width // 8):
            start = pl.multiple_of(j * width + h * 8, 8)
            rows = pl.ds(start, 8)
            wide = lambda x: jnp.concatenate([x] * (axial // LANES), axis=1)
            fac = [wide(factor[t, pl.ds(start + PAD, 8), :]) for t in range(2)]
            prev = [wide(pair[t, 0, rows, :]) for t in range(2)]
            succ = [wide(pair[t, 1, rows, :]) for t in range(2)]
            for p in range(planes):
                q, force = root[p, rows, :], load[p, rows, :]
                x0, x1 = field[0, p, rows, :], field[1, p, rows, :]
                images = [[None, None], [None, None]]
                for s, x in ((0, x0), (1, x1)):
                    tall = mixed[s, p, pl.ds(start + PAD - 8, 24), :]
                    up, centre, down = tall[7:15], tall[8:16], tall[9:17]
                    inner = (16.0 + SHIFT) * (q * x) - 2.0 * centre
                    for t in range(2):
                        im = q * (fac[t] * inner - (prev[t] * up + succ[t] * down))
                        image[t, s, p, rows, :] = im
                        images[t][s] = im
                for t in range(2):
                    i0, i1 = images[t]
                    add(8 * t + 0, x0 * i0)
                    add(8 * t + 1, x0 * i1)
                    add(8 * t + 2, x1 * i1)
                    add(8 * t + 3, force * i0)
                    add(8 * t + 4, force * i1)
                    add(8 * t + 5, i0 * i0)
                    add(8 * t + 6, i0 * i1)
                    add(8 * t + 7, i1 * i1)
                add(16, x0 * x0)
                add(17, x0 * x1)
                add(18, x1 * x1)
                add(19, force * x0)
                add(20, force * x1)
                add(21, force * force)
        for i in range(22):
            totals[i] += parts[i]
        return carry

    def step(tau, carry):
        for p in range(2):
            far_off = distance[p]
            k = tau - DEPTH * far_off

            @pl.when((k >= 0) & (k < pieces))
            def _():
                @pl.when(far_off > 0)
                def _():
                    hop(p, k).wait_recv()

                @pl.when(far_off < n_real - 1)
                def _():
                    hop(p, k).start()

                edge_hop(1, p, k).start()

        for p in range(2):
            @pl.when(tau < DEPTH)
            def _():
                sent[p, rows_of(tau), :] = own[plane_of(tau), place(p, tau), :]

            @pl.when((tau >= DEPTH) & (tau < slots_sent + DEPTH))
            def _():
                pass_on(p, tau - DEPTH).wait_recv()

            @pl.when((tau >= DEPTH) & (tau < slots_sent))
            def _():
                k = jnp.minimum(tau, pieces - 1)
                mine = own[plane_of(k), place(p, k), :]
                sent[p, rows_of(tau), :] = jnp.where(from_owner[p] == 0, mine, got[p, rows_of(tau - DEPTH), :])

            @pl.when(tau < slots_sent)
            def _():
                pass_on(p, tau).start()

            @pl.when((tau >= (n_real - 1) * DEPTH) & (tau < slots_sent + DEPTH))
            def _():
                k = tau - (n_real - 1) * DEPTH
                piece = own[plane_of(k), place(p, k), :]
                for d in range(1, n_real):
                    piece = jnp.where(from_owner[p] == d, got[p, rows_of(k + (d - 1) * DEPTH), :], piece)
                field[0, plane_of(k), place(p, k), :] = piece
                edge_hop(0, p, k).start()

        @pl.when(tau == 0)
        def _():
            prepare()

        done = tau - half - (n_real - 1) * DEPTH - LAG

        @pl.when(done == 0)
        def _():
            load_copy.wait()
            for p in range(2):
                root_hop(p).wait_recv()

        @pl.when(done >= 0)
        def _():
            for s in range(2):
                for p in range(2):
                    edge_arrives(s, p, done)
                    edge_arrives(s, p, half + done)
            lax.fori_loop(done * (ROWS // 8), (done + 1) * (ROWS // 8), mix, 0)
            per = ROWS // width
            first, end = jnp.maximum(done * per - 1, 1), (done + 1) * per - 1
            for p in range(2):
                lax.fori_loop(p * (sectors // 2) + first, p * (sectors // 2) + end, work, 0)

        return carry

    lax.fori_loop(0, pieces + (n_real - 1) * DEPTH + LAG, step, 0)

    for s in range(2):
        for p in range(2):
            mixed[s, p, 0:PAD, :] = mixed[s, p, circ : circ + PAD, :]
            mixed[s, p, circ + PAD : circ + 2 * PAD, :] = mixed[s, p, PAD : 2 * PAD, :]
    ends = sectors // 2 - 1
    lax.fori_loop(0, 4, lambda i, c: work(lax.div(i, 2) * (ends + 1) + lax.rem(i, 2) * ends, c), 0)

    lane = lax.broadcasted_iota(jnp.int32, (8, LANES), 1)
    packed = jnp.zeros((8, LANES), F32)
    for g in range(3):
        v = jnp.sum(totals[8 * g : 8 * g + 8], axis=1)
        v = v + pltpu.roll(v, 64, 1)
        v = v + pltpu.roll(v, 32, 1)
        packed = jnp.where((lane >= 32 * g) & (lane < 32 * g + 32), v, packed)

    def mate_hop(i, src, dst):
        return pltpu.make_async_remote_copy(
            src_ref=src,
            dst_ref=dst,
            send_sem=mate_send.at[i],
            recv_sem=mate_recv.at[i],
            device_id={"span": span + 1 - 2 * core},
            device_id_type=MESH,
        )

    def hub_hop(i):
        return pltpu.make_async_remote_copy(
            src_ref=mate.at[2],
            dst_ref=hub.at[i],
            send_sem=hub_send.at[i],
            recv_sem=hub_recv.at[i],
            device_id={"span": partner(i)},
            device_id_type=MESH,
        )

    mate[0] = packed
    first_meeting = mate_hop(0, mate.at[0], mate.at[1])
    first_meeting.start()
    first_meeting.wait_recv()
    mate[2] = mate[0] + mate[1]
    for i in range(hubs):
        @pl.when(core * hubs + i > 0)
        def _():
            hub_hop(i).start()

    @pl.when(core == 0)
    def _():
        hub[0] = mate[2]

    for i in range(hubs):
        @pl.when(core * hubs + i > 0)
        def _():
            hub_hop(i).wait_recv()

    far[core] = jnp.sum(hub[...], axis=0)
    last_meeting = mate_hop(1, far.at[core], far.at[core])
    last_meeting.start()
    last_meeting.wait_recv()

    for p in range(2):
        root_hop(p).wait_send()
    first_meeting.wait_send()
    last_meeting.wait_send()
    for i in range(hubs):
        @pl.when(core * hubs + i > 0)
        def _():
            hub_hop(i).wait_send()

    def whole(s, p, sem):
        return pltpu.make_async_copy(field.at[s, p], field.at[s, p], sem)

    for p in range(2):
        for s in range(2):
            whole(s, p, edge_send.at[s, p]).wait()

        @pl.when(distance[p] < n_real - 1)
        def _():
            whole(1, p, send_sem.at[p]).wait()

        pltpu.make_async_copy(sent.at[p], sent.at[p], sent_sem.at[p]).wait()


def finish_kernel(image, load, far, order, red, res, nrm, out, sems, *, cells):
    planes, circ, axial = load.shape
    group = lax.broadcasted_iota(jnp.int32, (1, LANES), 1) // 32
    rows = [far[:, r, :] for r in range(8)]

    def one(x, g):
        return jnp.sum(jnp.where(group == g, x, 0.0), axis=1, keepdims=True)

    def total(x):
        x = jnp.sum(x, axis=0, keepdims=True)
        return jnp.where(group == 0, one(x, 0), one(x, 1)) / cells

    def shared(x):
        return one(jnp.sum(x, axis=0, keepdims=True), 2) / cells

    swapped = order[0:1, :] > 0.5
    r00, r01, r11 = jnp.where(swapped, rows[2], rows[0]), rows[1], jnp.where(swapped, rows[0], rows[2])
    f0, f1 = jnp.where(swapped, rows[4], rows[3]), jnp.where(swapped, rows[3], rows[4])
    norm0 = shared(r00)
    along = shared(r01) / norm0
    rest = r11 - 2.0 * along * r01 + along * along * r00
    norm1 = shared(rest)
    inv0, inv1 = 1.0 / jnp.sqrt(norm0), 1.0 / jnp.sqrt(norm1)
    a00 = total(r00) * inv0 * inv0
    a01 = total(r01 - along * r00) * inv0 * inv1
    a11 = total(rest) * inv1 * inv1
    b0, b1 = shared(f0) * inv0, shared(f1 - along * f0) * inv1
    det = a00 * a11 - a01 * a01
    c0, c1 = (a11 * b0 - a01 * b1) / det, (a00 * b1 - a01 * b0) / det
    second = c1 * inv1
    first = c0 * inv0 - along * second
    g0, g1 = jnp.where(swapped, second, first), jnp.where(swapped, first, second)
    power = jnp.where(group == 0, pltpu.roll(rows[5], 64, 1), pltpu.roll(rows[5], 96, 1))
    square = total(
        power
        - 2.0 * (g0 * rows[3] + g1 * rows[4])
        + (g0 * g0 * rows[5] + 2.0 * g0 * g1 * rows[6] + g1 * g1 * rows[7])
    )
    spot = lax.broadcasted_iota(jnp.int32, (1, LANES), 1)

    scale = [[jnp.sum(jnp.where(spot == 32 * t, g, 0.0), axis=1, keepdims=True) for g in (g0, g1)] for t in range(2)]
    blocks = 8
    tall = circ // blocks

    def out_copy(t, b):
        rows = pl.ds(pl.multiple_of(b * tall, tall), tall)
        return pltpu.make_async_copy(out.at[t, :, rows], res.at[t, :, rows], sems.at[t])

    def finish(b, carry):
        def block(i, c):
            rows = pl.ds(pl.multiple_of(b * tall + i * 8, 8), 8)
            for p in range(planes):
                force = load[p, rows, :]
                for t in range(2):
                    out[t, p, rows, :] = force - (
                        scale[t][0] * image[t, 0, p, rows, :] + scale[t][1] * image[t, 1, p, rows, :]
                    )
            return c

        lax.fori_loop(0, tall // 8, block, 0)
        for t in range(2):
            out_copy(t, b).start()
        return carry

    lax.fori_loop(0, blocks, finish, 0)

    def scalar(x, t):
        return jnp.sum(jnp.where(spot == 32 * t, x, 0.0))

    for t in range(2):
        red[t, 0, 0] = scalar(a00, t)
        red[t, 0, 1] = scalar(a01, t)
        red[t, 1, 0] = scalar(a01, t)
        red[t, 1, 1] = scalar(a11, t)
        nrm[t] = scalar(square, t)

    for t in range(2):
        pltpu.make_async_copy(out.at[t], res.at[t], sems.at[t]).wait()


def shards(snapshots, load, base_modulus, mistune, material_ids, realization_map, picks):
    n_span, n_real = lax.axis_size("span"), lax.axis_size("real")
    held, planes, circ, axial = snapshots.shape
    hubs = n_span // 4
    pieces = circ // ROWS
    vmem = lambda *shape: pltpu.VMEM(shape, F32)
    dma = lambda *shape: pltpu.SemaphoreType.DMA(shape)

    kept = pieces + (n_real - 2) * DEPTH
    whole = lambda space, count: [pl.BlockSpec(memory_space=space)] * count
    sums = pl.pallas_call(
        gather_kernel,
        out_shape=(
            vmem(2, 2, planes, circ, axial),
            vmem(planes, circ, axial),
            vmem(2, 8, LANES),
            vmem(8, LANES),
        ),
        in_specs=whole(pltpu.HBM, 7),
        out_specs=tuple(whole(pltpu.VMEM, 4)),
        scratch_shapes=[
            pltpu.SMEM(picks.shape, jnp.int32),
            pltpu.SMEM(mistune.shape, F32),
            pltpu.SMEM(material_ids.shape, jnp.int32),
            pltpu.SMEM(realization_map.shape, jnp.int32),
            vmem(2, planes, circ, axial),
            vmem(2, 2, circ, axial),
            vmem(held, planes, circ, axial),
            vmem(planes, circ, axial),
            vmem(planes, kept * ROWS, axial),
            vmem(planes, kept * ROWS, axial),
            vmem(planes, circ, axial),
            vmem(2, circ, axial),
            vmem(2, planes, circ + 2 * PAD, axial),
            vmem(2, circ + 2 * PAD, LANES),
            vmem(2, 2, circ, LANES),
            vmem(24, 8, LANES),
            vmem(3, 8, LANES),
            vmem(hubs, 8, LANES),
            dma(4),
            dma(4),
            dma(2),
            dma(2, pieces),
            dma(2),
            dma(2, kept),
            dma(2, 2),
            dma(2, 2, pieces),
            dma(2),
            dma(2),
            dma(2),
            dma(2),
            dma(hubs),
            dma(hubs),
        ],
        compiler_params=pltpu.CompilerParams(
            collective_id=0, has_side_effects=True, vmem_limit_bytes=58720256
        ),
    )(picks, mistune, material_ids, realization_map, snapshots, load, base_modulus)
    return pl.pallas_call(
        functools.partial(finish_kernel, cells=float(planes * n_span * circ * axial)),
        out_shape=(
            jax.ShapeDtypeStruct((2, 2, 2), F32),
            jax.ShapeDtypeStruct((2, planes, circ, axial), F32),
            jax.ShapeDtypeStruct((2,), F32),
        ),
        in_specs=whole(pltpu.VMEM, 4),
        out_specs=(
            pl.BlockSpec(memory_space=pltpu.SMEM),
            pl.BlockSpec(memory_space=pltpu.HBM),
            pl.BlockSpec(memory_space=pltpu.SMEM),
        ),
        scratch_shapes=[vmem(2, planes, circ, axial), dma(2)],
        compiler_params=pltpu.CompilerParams(vmem_limit_bytes=40 * 2**20),
    )(*sums)


def solution(mesh):
    return jax.shard_map(
        shards,
        mesh=mesh,
        in_specs=(
            P("real", "span", None, None),
            P("span", None, None),
            P("span", None, None),
            P(),
            P(),
            P("real"),
            P(),
        ),
        out_specs=(P("real", None, None), P("real", "span", None, None), P("real")),
        check_vma=False,
    )
```

```python
import functools

import jax
import jax.numpy as jnp
from jax import lax
from jax.experimental import pallas as pl
from jax.experimental.pallas import tpu as pltpu
from jax.sharding import PartitionSpec as P

MESH = pl.DeviceIdType.MESH
SHIFT = 0.5
ROWS = 32
DEPTH = 3
LAG = 1
PAD = 8
LANES = 128
F32 = jnp.float32


def gather_kernel(
    picks_in, mistune_in, ids_in, slots_in, snaps, load_in, base_in,
    image, load, far, order,
    picks, mistune, ids, slots,
    field, edge, both, own, sent, got, root, root_edge, mixed, factor, pair, totals, mate, hub,
    small_sem, local_sem, send_sem, recv_sem, sent_sem, got_sem, edge_send, edge_recv, root_send, root_recv,
    mate_send, mate_recv, hub_send, hub_recv,
):
    n_span, n_real = lax.axis_size("span"), lax.axis_size("real")
    span, real = lax.axis_index("span"), lax.axis_index("real")
    held, planes, circ, axial = snaps.shape
    sectors = ids_in.shape[1]
    width = circ // sectors
    pieces = circ // ROWS
    last = held * n_real - 1
    slots_sent = pieces + (n_real - 2) * DEPTH
    before, after = lax.rem(span + n_span - 1, n_span), lax.rem(span + 1, n_span)
    below, above = lax.rem(real + n_real - 1, n_real), lax.rem(real + 1, n_real)
    core, chip, chips = lax.rem(span, 2), lax.div(span, 2), n_span // 2
    outer, inner = core, 1 - core
    hubs = chips

    def partner(step):
        return 2 * lax.rem(chip + step, chips) + core

    barrier = pltpu.get_barrier_semaphore()
    for where in [{"real": below}, {"real": above}, {"span": before}, {"span": after}]:
        pl.semaphore_signal(barrier, inc=1, device_id=where, device_id_type=MESH)
    for i in range(1, hubs):
        source = 2 * lax.rem(chip + chips - i, chips) + core

        pl.semaphore_signal(barrier, inc=1, device_id={"span": source}, device_id_type=MESH)

    smalls = [
        pltpu.make_async_copy(src, dst, small_sem.at[i])
        for i, (src, dst) in enumerate(((picks_in, picks), (mistune_in, mistune), (ids_in, ids), (slots_in, slots)))
    ]
    base_copy = pltpu.make_async_copy(base_in, root, local_sem.at[0])
    load_copy = pltpu.make_async_copy(load_in, load, local_sem.at[1])
    last_copy = pltpu.make_async_copy(snaps.at[held - 1], field.at[1], local_sem.at[2])
    both_copy = pltpu.make_async_copy(snaps, both, local_sem.at[3])
    for copy in smalls:
        copy.start()
    base_copy.start()
    both_copy.start()

    @pl.when(real == n_real - 1)
    def _():
        last_copy.start()

    load_copy.start()
    for copy in smalls:
        copy.wait()
    other = jnp.minimum(picks[0], picks[1])
    order[...] = jnp.full(order.shape, jnp.where(picks[0] == last, 1.0, 0.0), F32)

    both_copy.wait()
    chosen = lax.rem(other, held)

    def choose_own(i, carry):
        rows = pl.ds(pl.multiple_of(i * 16, 16), 16)
        for p in range(planes):
            own[p, rows, :] = jnp.where(chosen == 0, both[0, p, rows, :], both[held - 1, p, rows, :])
        return carry

    lax.fori_loop(0, circ // 16, choose_own, 0)

    @pl.when(real == n_real - 1)
    def _():
        last_copy.wait()

    pl.semaphore_wait(barrier, 4 + hubs - 1)

    def root_hop(p):
        return pltpu.make_async_remote_copy(
            src_ref=root.at[p],
            dst_ref=root_edge.at[1 - p],
            send_sem=root_send.at[p],
            recv_sem=root_recv.at[1 - p],
            device_id={"span": before if p == 0 else after},
            device_id_type=MESH,
        )

    def rows_of(k):
        return pl.ds(pl.multiple_of(k * ROWS, ROWS), ROWS)

    half = pieces // 2

    def plane_of(k):
        return jnp.where(k < half, outer, inner)

    def place(p, k):
        return rows_of(p * half + lax.rem(k, half))

    def prepare():
        base_copy.wait()

        def take_root(i, carry):
            rows = pl.ds(pl.multiple_of(i * 16, 16), 16)
            for p in range(planes):
                root[p, rows, :] = jnp.sqrt(root[p, rows, :])
            return carry

        lax.fori_loop(0, circ // 16, take_root, 0)
        for p in range(2):
            root_hop(p).start()

        def fill(j, carry):
            for t in range(2):
                value = mistune[ids[slots[t], j]]
                factor[t, pl.ds(PAD + j * width, width), :] = jnp.full((width, LANES), value, F32)
            return carry

        lax.fori_loop(0, sectors, fill, 0)
        for t in range(2):
            factor[t, 0:PAD, :] = factor[t, circ : circ + PAD, :]
            factor[t, circ + PAD : circ + 2 * PAD, :] = factor[t, PAD : 2 * PAD, :]
            here = factor[t, PAD : circ + PAD, :]
            for side, shift in ((0, -1), (1, 1)):
                pair[t, side] = jnp.sqrt(here * factor[t, PAD + shift : circ + PAD + shift, :])
        totals[...] = jnp.zeros_like(totals)

    def along(p):
        return {"real": above if p == 0 else below}

    def hop(p, k):
        return pltpu.make_async_remote_copy(
            src_ref=field.at[1, plane_of(k), place(p, k)],
            dst_ref=field.at[1, plane_of(k), place(p, k)],
            send_sem=send_sem.at[p],
            recv_sem=recv_sem.at[p, k],
            device_id=along(p),
            device_id_type=MESH,
        )

    def pass_on(p, k):
        return pltpu.make_async_remote_copy(
            src_ref=sent.at[p, rows_of(k)],
            dst_ref=got.at[p, rows_of(k)],
            send_sem=sent_sem.at[p],
            recv_sem=got_sem.at[p, k],
            device_id=along(p),
            device_id_type=MESH,
        )

    def edge_hop(s, p, k):
        plane = plane_of(k)
        return pltpu.make_async_remote_copy(
            src_ref=field.at[s, plane, place(p, k)],
            dst_ref=edge.at[s, 1 - plane, place(p, k)],
            send_sem=edge_send.at[s, p],
            recv_sem=edge_recv.at[s, p, k],
            device_id={"span": jnp.where(plane == 0, before, after)},
            device_id_type=MESH,
        )

    def edge_arrives(s, p, k):
        here = edge.at[s, plane_of(k), place(p, k)]
        pltpu.make_async_copy(here, here, edge_recv.at[s, p, k]).wait()

    distance = (real + 1) % n_real, n_real - 1 - real
    owner = lax.div(other, held)
    from_owner = (lax.rem(real + n_real - owner, n_real), lax.rem(owner + n_real - real, n_real))

    low = jnp.where(span > 0, 0.5, 0.0).astype(F32)
    high = jnp.where(span < n_span - 1, 0.5, 0.0).astype(F32)
    column = lax.broadcasted_iota(jnp.int32, (8, axial), 1)
    not_first, not_last = column > 0, column < axial - 1

    def mix(k, carry):
        for p in range(2):
            mix_rows(pl.multiple_of(p * (circ // 2) + k * 8, 8))
        return carry

    def mix_rows(start):
        rows = pl.ds(start, 8)
        q0, q1, ql, qh = root[0, rows, :], root[1, rows, :], root_edge[0, rows, :], root_edge[1, rows, :]
        for s in range(2):
            w0, w1 = q0 * field[s, 0, rows, :], q1 * field[s, 1, rows, :]
            wl, wh = ql * edge[s, 0, rows, :], qh * edge[s, 1, rows, :]
            for p, across in ((0, w0 + (low * wl + 0.5 * w1)), (1, w1 + (high * wh + 0.5 * w0))):
                left = jnp.where(not_first, pltpu.roll(across, 1, 1), 0.0)
                right = jnp.where(not_last, pltpu.roll(across, axial - 1, 1), 0.0)
                mixed[s, p, pl.ds(start + PAD, 8), :] = across + 0.5 * (left + right)

    def fold(x):
        return x[:, :LANES] + x[:, LANES:]

    def work(j, carry):
        parts = [None] * 22

        def add(i, x):
            x = fold(x)
            parts[i] = x if parts[i] is None else parts[i] + x

        for h in range(width // 8):
            start = pl.multiple_of(j * width + h * 8, 8)
            rows = pl.ds(start, 8)
            wide = lambda x: jnp.concatenate([x] * (axial // LANES), axis=1)
            fac = [wide(factor[t, pl.ds(start + PAD, 8), :]) for t in range(2)]
            prev = [wide(pair[t, 0, rows, :]) for t in range(2)]
            succ = [wide(pair[t, 1, rows, :]) for t in range(2)]
            for p in range(planes):
                q, force = root[p, rows, :], load[p, rows, :]
                x0, x1 = field[0, p, rows, :], field[1, p, rows, :]
                images = [[None, None], [None, None]]
                for s, x in ((0, x0), (1, x1)):
                    tall = mixed[s, p, pl.ds(start + PAD - 8, 24), :]
                    up, centre, down = tall[7:15], tall[8:16], tall[9:17]
                    inner = (16.0 + SHIFT) * (q * x) - 2.0 * centre
                    for t in range(2):
                        im = q * (fac[t] * inner - (prev[t] * up + succ[t] * down))
                        image[t, s, p, rows, :] = im
                        images[t][s] = im
                for t in range(2):
                    i0, i1 = images[t]
                    add(8 * t + 0, x0 * i0)
                    add(8 * t + 1, x0 * i1)
                    add(8 * t + 2, x1 * i1)
                    add(8 * t + 3, force * i0)
                    add(8 * t + 4, force * i1)
                    add(8 * t + 5, i0 * i0)
                    add(8 * t + 6, i0 * i1)
                    add(8 * t + 7, i1 * i1)
                add(16, x0 * x0)
                add(17, x0 * x1)
                add(18, x1 * x1)
                add(19, force * x0)
                add(20, force * x1)
                add(21, force * force)
        for i in range(22):
            totals[i] += parts[i]
        return carry

    def step(tau, carry):
        for p in range(2):
            @pl.when(tau < DEPTH)
            def _():
                sent[p, rows_of(tau), :] = own[plane_of(tau), place(p, tau), :]

            @pl.when((tau >= DEPTH) & (tau < slots_sent + DEPTH))
            def _():
                pass_on(p, tau - DEPTH).wait_recv()

            @pl.when((tau >= DEPTH) & (tau < slots_sent))
            def _():
                k = jnp.minimum(tau, pieces - 1)
                mine = own[plane_of(k), place(p, k), :]
                sent[p, rows_of(tau), :] = jnp.where(from_owner[p] == 0, mine, got[p, rows_of(tau - DEPTH), :])

            @pl.when(tau < slots_sent)
            def _():
                pass_on(p, tau).start()

            @pl.when((tau >= (n_real - 1) * DEPTH) & (tau < slots_sent + DEPTH))
            def _():
                k = tau - (n_real - 1) * DEPTH
                piece = own[plane_of(k), place(p, k), :]
                for d in range(1, n_real):
                    piece = jnp.where(from_owner[p] == d, got[p, rows_of(k + (d - 1) * DEPTH), :], piece)
                field[0, plane_of(k), place(p, k), :] = piece
                edge_hop(0, p, k).start()

        for p in range(2):
            far_off = distance[p]
            k = tau - DEPTH * far_off

            @pl.when((k >= 0) & (k < pieces))
            def _():
                @pl.when(far_off > 0)
                def _():
                    hop(p, k).wait_recv()

                @pl.when(far_off < n_real - 1)
                def _():
                    hop(p, k).start()

                edge_hop(1, p, k).start()

        @pl.when(tau == 0)
        def _():
            prepare()

        done = tau - half - (n_real - 1) * DEPTH - LAG

        @pl.when(done == 0)
        def _():
            load_copy.wait()
            for p in range(2):
                root_hop(p).wait_recv()

        @pl.when(done >= 0)
        def _():
            for s in range(2):
                for p in range(2):
                    edge_arrives(s, p, done)
                    edge_arrives(s, p, half + done)
            lax.fori_loop(done * (ROWS // 8), (done + 1) * (ROWS // 8), mix, 0)
            per = ROWS // width
            first, end = jnp.maximum(done * per - 1, 1), (done + 1) * per - 1
            for p in range(2):
                lax.fori_loop(p * (sectors // 2) + first, p * (sectors // 2) + end, work, 0)

        return carry

    lax.fori_loop(0, pieces + (n_real - 1) * DEPTH + LAG, step, 0)

    for s in range(2):
        for p in range(2):
            mixed[s, p, 0:PAD, :] = mixed[s, p, circ : circ + PAD, :]
            mixed[s, p, circ + PAD : circ + 2 * PAD, :] = mixed[s, p, PAD : 2 * PAD, :]
    ends = sectors // 2 - 1
    lax.fori_loop(0, 4, lambda i, c: work(lax.div(i, 2) * (ends + 1) + lax.rem(i, 2) * ends, c), 0)

    lane = lax.broadcasted_iota(jnp.int32, (8, LANES), 1)
    packed = jnp.zeros((8, LANES), F32)
    for g in range(3):
        v = jnp.sum(totals[8 * g : 8 * g + 8], axis=1)
        v = v + pltpu.roll(v, 64, 1)
        v = v + pltpu.roll(v, 32, 1)
        packed = jnp.where((lane >= 32 * g) & (lane < 32 * g + 32), v, packed)

    def mate_hop(i, src, dst):
        return pltpu.make_async_remote_copy(
            src_ref=src,
            dst_ref=dst,
            send_sem=mate_send.at[i],
            recv_sem=mate_recv.at[i],
            device_id={"span": span + 1 - 2 * core},
            device_id_type=MESH,
        )

    def hub_hop(i):
        return pltpu.make_async_remote_copy(
            src_ref=mate.at[2],
            dst_ref=hub.at[i],
            send_sem=hub_send.at[i],
            recv_sem=hub_recv.at[i],
            device_id={"span": partner(i)},
            device_id_type=MESH,
        )

    mate[0] = packed
    first_meeting = mate_hop(0, mate.at[0], mate.at[1])
    first_meeting.start()
    first_meeting.wait_recv()
    mate[2] = mate[0] + mate[1]
    for i in range(1, hubs):
        hub_hop(i).start()

    hub[0] = mate[2]

    for i in range(1, hubs):
        hub_hop(i).wait_recv()

    far[0] = jnp.sum(hub[...], axis=0)

    for p in range(2):
        root_hop(p).wait_send()
    first_meeting.wait_send()
    for i in range(1, hubs):
        hub_hop(i).wait_send()

    def whole(s, p, sem):
        return pltpu.make_async_copy(field.at[s, p], field.at[s, p], sem)

    for p in range(2):
        for s in range(2):
            whole(s, p, edge_send.at[s, p]).wait()

        @pl.when(distance[p] < n_real - 1)
        def _():
            whole(1, p, send_sem.at[p]).wait()

        pltpu.make_async_copy(sent.at[p], sent.at[p], sent_sem.at[p]).wait()


def finish_kernel(image, load, far, order, red, res, nrm, out, sems, *, cells):
    planes, circ, axial = load.shape
    group = lax.broadcasted_iota(jnp.int32, (1, LANES), 1) // 32
    rows = [far[:, r, :] for r in range(8)]

    def one(x, g):
        return jnp.sum(jnp.where(group == g, x, 0.0), axis=1, keepdims=True)

    def total(x):
        x = jnp.sum(x, axis=0, keepdims=True)
        return jnp.where(group == 0, one(x, 0), one(x, 1)) / cells

    def shared(x):
        return one(jnp.sum(x, axis=0, keepdims=True), 2) / cells

    swapped = order[0:1, :] > 0.5
    r00, r01, r11 = jnp.where(swapped, rows[2], rows[0]), rows[1], jnp.where(swapped, rows[0], rows[2])
    f0, f1 = jnp.where(swapped, rows[4], rows[3]), jnp.where(swapped, rows[3], rows[4])
    norm0 = shared(r00)
    along = shared(r01) / norm0
    rest = r11 - 2.0 * along * r01 + along * along * r00
    norm1 = shared(rest)
    inv0, inv1 = 1.0 / jnp.sqrt(norm0), 1.0 / jnp.sqrt(norm1)
    a00 = total(r00) * inv0 * inv0
    a01 = total(r01 - along * r00) * inv0 * inv1
    a11 = total(rest) * inv1 * inv1
    b0, b1 = shared(f0) * inv0, shared(f1 - along * f0) * inv1
    det = a00 * a11 - a01 * a01
    c0, c1 = (a11 * b0 - a01 * b1) / det, (a00 * b1 - a01 * b0) / det
    second = c1 * inv1
    first = c0 * inv0 - along * second
    g0, g1 = jnp.where(swapped, second, first), jnp.where(swapped, first, second)
    power = jnp.where(group == 0, pltpu.roll(rows[5], 64, 1), pltpu.roll(rows[5], 96, 1))
    square = total(
        power
        - 2.0 * (g0 * rows[3] + g1 * rows[4])
        + (g0 * g0 * rows[5] + 2.0 * g0 * g1 * rows[6] + g1 * g1 * rows[7])
    )
    spot = lax.broadcasted_iota(jnp.int32, (1, LANES), 1)

    scale = [[jnp.sum(jnp.where(spot == 32 * t, g, 0.0), axis=1, keepdims=True) for g in (g0, g1)] for t in range(2)]
    blocks = 8
    tall = circ // blocks

    def out_copy(t, b):
        rows = pl.ds(pl.multiple_of(b * tall, tall), tall)
        return pltpu.make_async_copy(out.at[t, :, rows], res.at[t, :, rows], sems.at[t])

    def finish(b, carry):
        def block(i, c):
            rows = pl.ds(pl.multiple_of(b * tall + i * 8, 8), 8)
            for p in range(planes):
                force = load[p, rows, :]
                for t in range(2):
                    out[t, p, rows, :] = force - (
                        scale[t][0] * image[t, 0, p, rows, :] + scale[t][1] * image[t, 1, p, rows, :]
                    )
            return c

        lax.fori_loop(0, tall // 8, block, 0)
        for t in range(2):
            out_copy(t, b).start()
        return carry

    lax.fori_loop(0, blocks, finish, 0)

    def scalar(x, t):
        return jnp.sum(jnp.where(spot == 32 * t, x, 0.0))

    for t in range(2):
        red[t, 0, 0] = scalar(a00, t)
        red[t, 0, 1] = scalar(a01, t)
        red[t, 1, 0] = scalar(a01, t)
        red[t, 1, 1] = scalar(a11, t)
        nrm[t] = scalar(square, t)

    for t in range(2):
        pltpu.make_async_copy(out.at[t], res.at[t], sems.at[t]).wait()


def shards(snapshots, load, base_modulus, mistune, material_ids, realization_map, picks):
    n_span, n_real = lax.axis_size("span"), lax.axis_size("real")
    held, planes, circ, axial = snapshots.shape
    hubs = n_span // 2
    pieces = circ // ROWS
    vmem = lambda *shape: pltpu.VMEM(shape, F32)
    dma = lambda *shape: pltpu.SemaphoreType.DMA(shape)

    kept = pieces + (n_real - 2) * DEPTH
    whole = lambda space, count: [pl.BlockSpec(memory_space=space)] * count
    sums = pl.pallas_call(
        gather_kernel,
        out_shape=(
            vmem(2, 2, planes, circ, axial),
            vmem(planes, circ, axial),
            vmem(1, 8, LANES),
            vmem(8, LANES),
        ),
        in_specs=whole(pltpu.HBM, 7),
        out_specs=tuple(whole(pltpu.VMEM, 4)),
        scratch_shapes=[
            pltpu.SMEM(picks.shape, jnp.int32),
            pltpu.SMEM(mistune.shape, F32),
            pltpu.SMEM(material_ids.shape, jnp.int32),
            pltpu.SMEM(realization_map.shape, jnp.int32),
            vmem(2, planes, circ, axial),
            vmem(2, 2, circ, axial),
            vmem(held, planes, circ, axial),
            vmem(planes, circ, axial),
            vmem(planes, kept * ROWS, axial),
            vmem(planes, kept * ROWS, axial),
            vmem(planes, circ, axial),
            vmem(2, circ, axial),
            vmem(2, planes, circ + 2 * PAD, axial),
            vmem(2, circ + 2 * PAD, LANES),
            vmem(2, 2, circ, LANES),
            vmem(24, 8, LANES),
            vmem(3, 8, LANES),
            vmem(hubs, 8, LANES),
            dma(4),
            dma(4),
            dma(2),
            dma(2, pieces),
            dma(2),
            dma(2, kept),
            dma(2, 2),
            dma(2, 2, pieces),
            dma(2),
            dma(2),
            dma(1),
            dma(1),
            dma(hubs),
            dma(hubs),
        ],
        compiler_params=pltpu.CompilerParams(
            collective_id=0, has_side_effects=True, vmem_limit_bytes=58720256
        ),
    )(picks, mistune, material_ids, realization_map, snapshots, load, base_modulus)
    return pl.pallas_call(
        functools.partial(finish_kernel, cells=float(planes * n_span * circ * axial)),
        out_shape=(
            jax.ShapeDtypeStruct((2, 2, 2), F32),
            jax.ShapeDtypeStruct((2, planes, circ, axial), F32),
            jax.ShapeDtypeStruct((2,), F32),
        ),
        in_specs=whole(pltpu.VMEM, 4),
        out_specs=(
            pl.BlockSpec(memory_space=pltpu.SMEM),
            pl.BlockSpec(memory_space=pltpu.HBM),
            pl.BlockSpec(memory_space=pltpu.SMEM),
        ),
        scratch_shapes=[vmem(2, planes, circ, axial), dma(2)],
        compiler_params=pltpu.CompilerParams(vmem_limit_bytes=40 * 2**20),
    )(*sums)


def solution(mesh):
    return jax.shard_map(
        shards,
        mesh=mesh,
        in_specs=(
            P("real", "span", None, None),
            P("span", None, None),
            P("span", None, None),
            P(),
            P(),
            P("real"),
            P(),
        ),
        out_specs=(P("real", None, None), P("real", "span", None, None), P("real")),
        check_vma=False,
    )
```

```python
import functools

import jax
import jax.numpy as jnp
from jax import lax
from jax.experimental import pallas as pl
from jax.experimental.pallas import tpu as pltpu
from jax.sharding import PartitionSpec as P

MESH = pl.DeviceIdType.MESH
SHIFT = 0.5
ROWS = 32
DEPTH = 3
LAG = 1
PAD = 8
LANES = 128
F32 = jnp.float32


def gather_kernel(
    picks_in, mistune_in, ids_in, slots_in, snaps, load_in, base_in,
    image, load, far, order,
    picks, mistune, ids, slots,
    field, edge, both, own, sent, got, root, root_edge, mixed, factor, pair, totals, mate, hub,
    small_sem, local_sem, send_sem, recv_sem, sent_sem, got_sem, edge_send, edge_recv, root_send, root_recv,
    mate_send, mate_recv, hub_send, hub_recv,
):
    n_span, n_real = lax.axis_size("span"), lax.axis_size("real")
    span, real = lax.axis_index("span"), lax.axis_index("real")
    held, planes, circ, axial = snaps.shape
    sectors = ids_in.shape[1]
    width = circ // sectors
    pieces = circ // ROWS
    last = held * n_real - 1
    slots_sent = pieces + (n_real - 2) * DEPTH
    before, after = lax.rem(span + n_span - 1, n_span), lax.rem(span + 1, n_span)
    below, above = lax.rem(real + n_real - 1, n_real), lax.rem(real + 1, n_real)
    core, chip, chips = lax.rem(span, 2), lax.div(span, 2), n_span // 2
    outer, inner = core, 1 - core
    hubs = chips

    def partner(step):
        return 2 * lax.rem(chip + step, chips) + core

    barrier = pltpu.get_barrier_semaphore()
    for where in [{"real": below}, {"real": above}, {"span": before}, {"span": after}]:
        pl.semaphore_signal(barrier, inc=1, device_id=where, device_id_type=MESH)
    for i in range(1, hubs):
        source = 2 * lax.rem(chip + chips - i, chips) + core

        pl.semaphore_signal(barrier, inc=1, device_id={"span": source}, device_id_type=MESH)

    smalls = [
        pltpu.make_async_copy(src, dst, small_sem.at[i])
        for i, (src, dst) in enumerate(((picks_in, picks), (mistune_in, mistune), (ids_in, ids), (slots_in, slots)))
    ]
    base_copy = pltpu.make_async_copy(base_in, root, local_sem.at[0])
    load_copy = pltpu.make_async_copy(load_in, load, local_sem.at[1])
    last_copy = pltpu.make_async_copy(snaps.at[held - 1], field.at[1], local_sem.at[2])
    both_copy = pltpu.make_async_copy(snaps, both, local_sem.at[3])
    for copy in smalls:
        copy.start()
    base_copy.start()
    both_copy.start()

    @pl.when(real == n_real - 1)
    def _():
        last_copy.start()

    load_copy.start()
    for copy in smalls:
        copy.wait()
    other = jnp.minimum(picks[0], picks[1])
    order[...] = jnp.full(order.shape, jnp.where(picks[0] == last, 1.0, 0.0), F32)

    both_copy.wait()
    chosen = lax.rem(other, held)

    def choose_own(i, carry):
        rows = pl.ds(pl.multiple_of(i * 16, 16), 16)
        for p in range(planes):
            own[p, rows, :] = jnp.where(chosen == 0, both[0, p, rows, :], both[held - 1, p, rows, :])
        return carry

    lax.fori_loop(0, circ // 16, choose_own, 0, unroll=4)

    @pl.when(real == n_real - 1)
    def _():
        last_copy.wait()

    pl.semaphore_wait(barrier, 4 + hubs - 1)

    def root_hop(p):
        return pltpu.make_async_remote_copy(
            src_ref=root.at[p],
            dst_ref=root_edge.at[1 - p],
            send_sem=root_send.at[p],
            recv_sem=root_recv.at[1 - p],
            device_id={"span": before if p == 0 else after},
            device_id_type=MESH,
        )

    def rows_of(k):
        return pl.ds(pl.multiple_of(k * ROWS, ROWS), ROWS)

    half = pieces // 2

    def plane_of(k):
        return jnp.where(k < half, outer, inner)

    def place(p, k):
        return rows_of(p * half + lax.rem(k, half))

    def prepare():
        base_copy.wait()

        def take_root(i, carry):
            rows = pl.ds(pl.multiple_of(i * 16, 16), 16)
            for p in range(planes):
                root[p, rows, :] = jnp.sqrt(root[p, rows, :])
            return carry

        lax.fori_loop(0, circ // 16, take_root, 0, unroll=4)
        for p in range(2):
            root_hop(p).start()

        def fill(j, carry):
            for t in range(2):
                value = mistune[ids[slots[t], j]]
                factor[t, pl.ds(PAD + j * width, width), :] = jnp.full((width, LANES), value, F32)
            return carry

        lax.fori_loop(0, sectors, fill, 0)
        for t in range(2):
            factor[t, 0:PAD, :] = factor[t, circ : circ + PAD, :]
            factor[t, circ + PAD : circ + 2 * PAD, :] = factor[t, PAD : 2 * PAD, :]
            here = factor[t, PAD : circ + PAD, :]
            for side, shift in ((0, -1), (1, 1)):
                pair[t, side] = jnp.sqrt(here * factor[t, PAD + shift : circ + PAD + shift, :])
        totals[...] = jnp.zeros_like(totals)

    def along(p):
        return {"real": above if p == 0 else below}

    def hop(p, k):
        return pltpu.make_async_remote_copy(
            src_ref=field.at[1, plane_of(k), place(p, k)],
            dst_ref=field.at[1, plane_of(k), place(p, k)],
            send_sem=send_sem.at[p],
            recv_sem=recv_sem.at[p, k],
            device_id=along(p),
            device_id_type=MESH,
        )

    def pass_on(p, k):
        return pltpu.make_async_remote_copy(
            src_ref=sent.at[p, rows_of(k)],
            dst_ref=got.at[p, rows_of(k)],
            send_sem=sent_sem.at[p],
            recv_sem=got_sem.at[p, k],
            device_id=along(p),
            device_id_type=MESH,
        )

    def edge_hop(s, p, k):
        plane = plane_of(k)
        return pltpu.make_async_remote_copy(
            src_ref=field.at[s, plane, place(p, k)],
            dst_ref=edge.at[s, 1 - plane, place(p, k)],
            send_sem=edge_send.at[s, p],
            recv_sem=edge_recv.at[s, p, k],
            device_id={"span": jnp.where(plane == 0, before, after)},
            device_id_type=MESH,
        )

    def edge_arrives(s, p, k):
        here = edge.at[s, plane_of(k), place(p, k)]
        pltpu.make_async_copy(here, here, edge_recv.at[s, p, k]).wait()

    distance = (real + 1) % n_real, n_real - 1 - real
    owner = lax.div(other, held)
    from_owner = (lax.rem(real + n_real - owner, n_real), lax.rem(owner + n_real - real, n_real))

    low = jnp.where(span > 0, 0.5, 0.0).astype(F32)
    high = jnp.where(span < n_span - 1, 0.5, 0.0).astype(F32)
    column = lax.broadcasted_iota(jnp.int32, (8, axial), 1)
    not_first, not_last = column > 0, column < axial - 1

    def mix(k, carry):
        for p in range(2):
            mix_rows(pl.multiple_of(p * (circ // 2) + k * 8, 8))
        return carry

    def mix_rows(start):
        rows = pl.ds(start, 8)
        q0, q1, ql, qh = root[0, rows, :], root[1, rows, :], root_edge[0, rows, :], root_edge[1, rows, :]
        for s in range(2):
            w0, w1 = q0 * field[s, 0, rows, :], q1 * field[s, 1, rows, :]
            wl, wh = ql * edge[s, 0, rows, :], qh * edge[s, 1, rows, :]
            for p, across in ((0, w0 + (low * wl + 0.5 * w1)), (1, w1 + (high * wh + 0.5 * w0))):
                left = jnp.where(not_first, pltpu.roll(across, 1, 1), 0.0)
                right = jnp.where(not_last, pltpu.roll(across, axial - 1, 1), 0.0)
                mixed[s, p, pl.ds(start + PAD, 8), :] = across + 0.5 * (left + right)

    def fold(x):
        return x[:, :LANES] + x[:, LANES:]

    def work(j, carry):
        parts = [None] * 22

        def add(i, x):
            x = fold(x)
            parts[i] = x if parts[i] is None else parts[i] + x

        for h in range(width // 8):
            start = pl.multiple_of(j * width + h * 8, 8)
            rows = pl.ds(start, 8)
            wide = lambda x: jnp.concatenate([x] * (axial // LANES), axis=1)
            fac = [wide(factor[t, pl.ds(start + PAD, 8), :]) for t in range(2)]
            prev = [wide(pair[t, 0, rows, :]) for t in range(2)]
            succ = [wide(pair[t, 1, rows, :]) for t in range(2)]
            for p in range(planes):
                q, force = root[p, rows, :], load[p, rows, :]
                x0, x1 = field[0, p, rows, :], field[1, p, rows, :]
                images = [[None, None], [None, None]]
                for s, x in ((0, x0), (1, x1)):
                    tall = mixed[s, p, pl.ds(start + PAD - 8, 24), :]
                    up, centre, down = tall[7:15], tall[8:16], tall[9:17]
                    inner = (16.0 + SHIFT) * (q * x) - 2.0 * centre
                    for t in range(2):
                        im = q * (fac[t] * inner - (prev[t] * up + succ[t] * down))
                        image[t, s, p, rows, :] = im
                        images[t][s] = im
                for t in range(2):
                    i0, i1 = images[t]
                    add(8 * t + 0, x0 * i0)
                    add(8 * t + 1, x0 * i1)
                    add(8 * t + 2, x1 * i1)
                    add(8 * t + 3, force * i0)
                    add(8 * t + 4, force * i1)
                    add(8 * t + 5, i0 * i0)
                    add(8 * t + 6, i0 * i1)
                    add(8 * t + 7, i1 * i1)
                add(16, x0 * x0)
                add(17, x0 * x1)
                add(18, x1 * x1)
                add(19, force * x0)
                add(20, force * x1)
                add(21, force * force)
        for i in range(22):
            totals[i] += parts[i]
        return carry

    def step(tau, carry):
        for p in range(2):
            @pl.when(tau < DEPTH)
            def _():
                sent[p, rows_of(tau), :] = own[plane_of(tau), place(p, tau), :]

            @pl.when((tau >= DEPTH) & (tau < slots_sent + DEPTH))
            def _():
                pass_on(p, tau - DEPTH).wait_recv()

            @pl.when((tau >= DEPTH) & (tau < slots_sent))
            def _():
                k = jnp.minimum(tau, pieces - 1)
                mine = own[plane_of(k), place(p, k), :]
                sent[p, rows_of(tau), :] = jnp.where(from_owner[p] == 0, mine, got[p, rows_of(tau - DEPTH), :])

            @pl.when(tau < slots_sent)
            def _():
                pass_on(p, tau).start()

            @pl.when((tau >= (n_real - 1) * DEPTH) & (tau < slots_sent + DEPTH))
            def _():
                k = tau - (n_real - 1) * DEPTH
                piece = own[plane_of(k), place(p, k), :]
                for d in range(1, n_real):
                    piece = jnp.where(from_owner[p] == d, got[p, rows_of(k + (d - 1) * DEPTH), :], piece)
                field[0, plane_of(k), place(p, k), :] = piece
                edge_hop(0, p, k).start()

        for p in range(2):
            far_off = distance[p]
            k = tau - DEPTH * far_off

            @pl.when((k >= 0) & (k < pieces))
            def _():
                @pl.when(far_off > 0)
                def _():
                    hop(p, k).wait_recv()

                @pl.when(far_off < n_real - 1)
                def _():
                    hop(p, k).start()

                edge_hop(1, p, k).start()

        @pl.when(tau == 0)
        def _():
            prepare()

        done = tau - half - (n_real - 1) * DEPTH - LAG

        @pl.when(done == 0)
        def _():
            load_copy.wait()
            for p in range(2):
                root_hop(p).wait_recv()

        @pl.when(done >= 0)
        def _():
            for s in range(2):
                for p in range(2):
                    edge_arrives(s, p, done)
                    edge_arrives(s, p, half + done)
            lax.fori_loop(0, ROWS // 8, lambda i, c: mix(done * (ROWS // 8) + i, c), 0, unroll=True)
            per = ROWS // width
            first, end = jnp.maximum(done * per - 1, 1), (done + 1) * per - 1
            for p in range(2):
                lax.fori_loop(p * (sectors // 2) + first, p * (sectors // 2) + end, work, 0)

        return carry

    lax.fori_loop(0, pieces + (n_real - 1) * DEPTH + LAG, step, 0)

    for s in range(2):
        for p in range(2):
            mixed[s, p, 0:PAD, :] = mixed[s, p, circ : circ + PAD, :]
            mixed[s, p, circ + PAD : circ + 2 * PAD, :] = mixed[s, p, PAD : 2 * PAD, :]
    ends = sectors // 2 - 1
    lax.fori_loop(0, 2, lambda i, c: work(i * (ends + 1) + ends, work(i * (ends + 1), c)), 0)

    lane = lax.broadcasted_iota(jnp.int32, (8, LANES), 1)
    packed = jnp.zeros((8, LANES), F32)
    for g in range(3):
        v = jnp.sum(totals[8 * g : 8 * g + 8], axis=1)
        v = v + pltpu.roll(v, 64, 1)
        v = v + pltpu.roll(v, 32, 1)
        packed = jnp.where((lane >= 32 * g) & (lane < 32 * g + 32), v, packed)

    def mate_hop(i, src, dst):
        return pltpu.make_async_remote_copy(
            src_ref=src,
            dst_ref=dst,
            send_sem=mate_send.at[i],
            recv_sem=mate_recv.at[i],
            device_id={"span": span + 1 - 2 * core},
            device_id_type=MESH,
        )

    def hub_hop(i):
        return pltpu.make_async_remote_copy(
            src_ref=mate.at[2],
            dst_ref=hub.at[i],
            send_sem=hub_send.at[i],
            recv_sem=hub_recv.at[i],
            device_id={"span": partner(i)},
            device_id_type=MESH,
        )

    mate[0] = packed
    first_meeting = mate_hop(0, mate.at[0], mate.at[1])
    first_meeting.start()
    first_meeting.wait_recv()
    mate[2] = mate[0] + mate[1]
    for i in range(1, hubs):
        hub_hop(i).start()

    hub[0] = mate[2]

    for i in range(1, hubs):
        hub_hop(i).wait_recv()

    far[0] = jnp.sum(hub[...], axis=0)

    for p in range(2):
        root_hop(p).wait_send()
    first_meeting.wait_send()
    for i in range(1, hubs):
        hub_hop(i).wait_send()

    def whole(s, p, sem):
        return pltpu.make_async_copy(field.at[s, p], field.at[s, p], sem)

    for p in range(2):
        for s in range(2):
            whole(s, p, edge_send.at[s, p]).wait()

        @pl.when(distance[p] < n_real - 1)
        def _():
            whole(1, p, send_sem.at[p]).wait()

        pltpu.make_async_copy(sent.at[p], sent.at[p], sent_sem.at[p]).wait()


def finish_kernel(image, load, far, order, red, res, nrm, out, sems, *, cells):
    planes, circ, axial = load.shape
    group = lax.broadcasted_iota(jnp.int32, (1, LANES), 1) // 32
    rows = [far[:, r, :] for r in range(8)]

    def one(x, g):
        return jnp.sum(jnp.where(group == g, x, 0.0), axis=1, keepdims=True)

    def total(x):
        x = jnp.sum(x, axis=0, keepdims=True)
        return jnp.where(group == 0, one(x, 0), one(x, 1)) / cells

    def shared(x):
        return one(jnp.sum(x, axis=0, keepdims=True), 2) / cells

    swapped = order[0:1, :] > 0.5
    r00, r01, r11 = jnp.where(swapped, rows[2], rows[0]), rows[1], jnp.where(swapped, rows[0], rows[2])
    f0, f1 = jnp.where(swapped, rows[4], rows[3]), jnp.where(swapped, rows[3], rows[4])
    norm0 = shared(r00)
    along = shared(r01) / norm0
    rest = r11 - 2.0 * along * r01 + along * along * r00
    norm1 = shared(rest)
    inv0, inv1 = 1.0 / jnp.sqrt(norm0), 1.0 / jnp.sqrt(norm1)
    a00 = total(r00) * inv0 * inv0
    a01 = total(r01 - along * r00) * inv0 * inv1
    a11 = total(rest) * inv1 * inv1
    b0, b1 = shared(f0) * inv0, shared(f1 - along * f0) * inv1
    det = a00 * a11 - a01 * a01
    c0, c1 = (a11 * b0 - a01 * b1) / det, (a00 * b1 - a01 * b0) / det
    second = c1 * inv1
    first = c0 * inv0 - along * second
    g0, g1 = jnp.where(swapped, second, first), jnp.where(swapped, first, second)
    power = jnp.where(group == 0, pltpu.roll(rows[5], 64, 1), pltpu.roll(rows[5], 96, 1))
    square = total(
        power
        - 2.0 * (g0 * rows[3] + g1 * rows[4])
        + (g0 * g0 * rows[5] + 2.0 * g0 * g1 * rows[6] + g1 * g1 * rows[7])
    )
    spot = lax.broadcasted_iota(jnp.int32, (1, LANES), 1)

    scale = [[jnp.sum(jnp.where(spot == 32 * t, g, 0.0), axis=1, keepdims=True) for g in (g0, g1)] for t in range(2)]
    blocks = 8
    tall = circ // blocks

    def out_copy(t, b):
        rows = pl.ds(pl.multiple_of(b * tall, tall), tall)
        return pltpu.make_async_copy(out.at[t, :, rows], res.at[t, :, rows], sems.at[t])

    def finish(b, carry):
        def block(i, c):
            rows = pl.ds(pl.multiple_of(b * tall + i * 8, 8), 8)
            for p in range(planes):
                force = load[p, rows, :]
                for t in range(2):
                    out[t, p, rows, :] = force - (
                        scale[t][0] * image[t, 0, p, rows, :] + scale[t][1] * image[t, 1, p, rows, :]
                    )
            return c

        lax.fori_loop(0, tall // 8, block, 0, unroll=True)
        for t in range(2):
            out_copy(t, b).start()
        return carry

    lax.fori_loop(0, blocks, finish, 0)

    def scalar(x, t):
        return jnp.sum(jnp.where(spot == 32 * t, x, 0.0))

    for t in range(2):
        red[t, 0, 0] = scalar(a00, t)
        red[t, 0, 1] = scalar(a01, t)
        red[t, 1, 0] = scalar(a01, t)
        red[t, 1, 1] = scalar(a11, t)
        nrm[t] = scalar(square, t)

    for t in range(2):
        pltpu.make_async_copy(out.at[t], res.at[t], sems.at[t]).wait()


def shards(snapshots, load, base_modulus, mistune, material_ids, realization_map, picks):
    n_span, n_real = lax.axis_size("span"), lax.axis_size("real")
    held, planes, circ, axial = snapshots.shape
    hubs = n_span // 2
    pieces = circ // ROWS
    vmem = lambda *shape: pltpu.VMEM(shape, F32)
    dma = lambda *shape: pltpu.SemaphoreType.DMA(shape)

    kept = pieces + (n_real - 2) * DEPTH
    whole = lambda space, count: [pl.BlockSpec(memory_space=space)] * count
    sums = pl.pallas_call(
        gather_kernel,
        out_shape=(
            vmem(2, 2, planes, circ, axial),
            vmem(planes, circ, axial),
            vmem(1, 8, LANES),
            vmem(8, LANES),
        ),
        in_specs=whole(pltpu.HBM, 7),
        out_specs=tuple(whole(pltpu.VMEM, 4)),
        scratch_shapes=[
            pltpu.SMEM(picks.shape, jnp.int32),
            pltpu.SMEM(mistune.shape, F32),
            pltpu.SMEM(material_ids.shape, jnp.int32),
            pltpu.SMEM(realization_map.shape, jnp.int32),
            vmem(2, planes, circ, axial),
            vmem(2, 2, circ, axial),
            vmem(held, planes, circ, axial),
            vmem(planes, circ, axial),
            vmem(planes, kept * ROWS, axial),
            vmem(planes, kept * ROWS, axial),
            vmem(planes, circ, axial),
            vmem(2, circ, axial),
            vmem(2, planes, circ + 2 * PAD, axial),
            vmem(2, circ + 2 * PAD, LANES),
            vmem(2, 2, circ, LANES),
            vmem(24, 8, LANES),
            vmem(3, 8, LANES),
            vmem(hubs, 8, LANES),
            dma(4),
            dma(4),
            dma(2),
            dma(2, pieces),
            dma(2),
            dma(2, kept),
            dma(2, 2),
            dma(2, 2, pieces),
            dma(2),
            dma(2),
            dma(1),
            dma(1),
            dma(hubs),
            dma(hubs),
        ],
        compiler_params=pltpu.CompilerParams(
            collective_id=0, has_side_effects=True, vmem_limit_bytes=58720256
        ),
    )(picks, mistune, material_ids, realization_map, snapshots, load, base_modulus)
    return pl.pallas_call(
        functools.partial(finish_kernel, cells=float(planes * n_span * circ * axial)),
        out_shape=(
            jax.ShapeDtypeStruct((2, 2, 2), F32),
            jax.ShapeDtypeStruct((2, planes, circ, axial), F32),
            jax.ShapeDtypeStruct((2,), F32),
        ),
        in_specs=whole(pltpu.VMEM, 4),
        out_specs=(
            pl.BlockSpec(memory_space=pltpu.SMEM),
            pl.BlockSpec(memory_space=pltpu.HBM),
            pl.BlockSpec(memory_space=pltpu.SMEM),
        ),
        scratch_shapes=[vmem(2, planes, circ, axial), dma(2)],
        compiler_params=pltpu.CompilerParams(vmem_limit_bytes=40 * 2**20),
    )(*sums)


def solution(mesh):
    return jax.shard_map(
        shards,
        mesh=mesh,
        in_specs=(
            P("real", "span", None, None),
            P("span", None, None),
            P("span", None, None),
            P(),
            P(),
            P("real"),
            P(),
        ),
        out_specs=(P("real", None, None), P("real", "span", None, None), P("real")),
        check_vma=False,
    )
```
